256 devices in a mesh: pipe: 8 (over y, x_hi), expert: 32 (over x_lo, z, core).
Axes of the slice: x: 4 (x_hi: 2, x_lo: 2; x = x_hi * 2 + x_lo), y: 4, z: 8, core: 2. Of those that a mesh axis runs over, the one named last changes fastest.
Arguments:
- fwd_state: bfloat16 [8, 1024, 3584], P('pipe', 'expert'), may hold values from -6 to 6
- new_tokens: bfloat16 [1, 1024, 3584], P(None, 'expert'), may hold values from -6 to 6
- saved_input: bfloat16 [2, 8, 1024, 3584], P(None, 'pipe', 'expert'), may hold values from -6 to 6
- grad_state: bfloat16 [8, 1024, 3584], P('pipe', 'expert'), may hold values from -6 to 6
- new_grads: bfloat16 [1, 1024, 3584], P(None, 'expert'), may hold values from -6 to 6
- norm_gain: float32 [8, 3584], P('pipe'), may hold values from 0.25 to 1.75
- w_gate: bfloat16 [8, 3584, 16384], P('pipe', None, 'expert'), may hold values from -0.09375 to 0.09375
- w_up: bfloat16 [8, 3584, 16384], P('pipe', None, 'expert'), may hold values from -0.09375 to 0.09375
- w_down: bfloat16 [8, 16384, 3584], P('pipe', 'expert'), may hold values from -0.1875 to 0.1875
- fwd_ids: int32 [2, 8, 1024, 4], P(None, 'pipe', 'expert'), may hold values from 0 to 15, all different within a row; in each aligned block of 32 rows (0 to 31, 32 to 63, ..., all dimensions but the last counted through in order) at most 8 rows name the same one
- fwd_gates: float32 [2, 8, 1024, 4], P(None, 'pipe', 'expert'), may hold values from 0.05 to 0.6
- bwd_ids: int32 [2, 8, 1024, 4], P(None, 'pipe', 'expert'), may hold values from 0 to 15, all different within a row; in each aligned block of 32 rows (0 to 31, 32 to 63, ..., all dimensions but the last counted through in order) at most 8 rows name the same one
- bwd_gates: float32 [2, 8, 1024, 4], P(None, 'pipe', 'expert'), may hold values from 0.05 to 0.6
Outputs:
- fwd_out: bfloat16 [8, 1024, 3584], P('pipe', 'expert')
- grad_out: bfloat16 [8, 1024, 3584], P('pipe', 'expert')
The draws below stay inside these ranges and needn't reach their ends.
Inputs may be any that keep to these rules, and one draw needn't show every extreme that they name: `fwd_ids`: each row names 4 different experts. In every aligned block of 32 rows (the tokens of one index of expert for one tick and layer) every expert is named by exactly 8 rows. `bwd_ids`: as for fwd_ids.
All inputs are finite; a program needn't handle non-finite values.
Results may differ from the reference program's by a relative error of at most 0.01.
Values may be sent and summed in bfloat16 or wider, within the bound.
A program may use at most 64 MiB of HBM per device.

```python
import math
import jax
import jax.numpy as jnp
import numpy as np
from jax import lax

D = 3584
HID = 1024
TOPK = 4
TICKS = 2
TOK_DEV = 32
EXPERTS = 16
LAYERS = 8
TOKENS = 1024
CAP = 8
N_EXPERT = 32


def block_levels(key, shape, split, smallest, largest):
    level = 1.0
    for dim, shards_of in split:
        draws = jax.random.uniform(jax.random.fold_in(jax.random.fold_in(key, 6), dim), (shards_of,), jnp.float32, smallest / len(split), largest / len(split))
        level = level * jnp.repeat(jnp.exp(draws), shape[dim] // shards_of).reshape((-1,) + (1,) * (len(shape) - 1 - dim))
    return level


def assign_block(stream_key, own, number, rows, amount, top, bound, lean):
    order = jax.random.permutation(stream_key, amount)
    packed, common = portions_of(amount, rows * top, bound, lean, True), portions_of(amount, rows * top, bound, lean, False)
    places = jnp.arange(amount)

    def named(lengths, offset_by):
        used = int((lengths > 0).sum())
        fixed = max(1, used // 4)
        passed = fixed + (places - fixed + offset_by * (used - fixed)) % max(1, amount - fixed)
        return jnp.zeros((amount,), jnp.int32).at[order[jnp.where(places < fixed, places, passed)]].set(jnp.asarray(lengths, jnp.int32))

    lengths = jnp.where(number % 4 == 0, named(packed, number // 4), named(common, number - number // 4 - 1))
    mixed = jax.random.permutation(jax.random.fold_in(own, 3), amount)
    giver, receiver = mixed[0:amount // 2 * 2:2], mixed[1:amount // 2 * 2:2]
    slack = jnp.minimum(lengths[giver] - 1, bound - lengths[receiver]) // 2
    slack = jnp.where((giver == order[0]) | (receiver == order[0]) | (lengths[receiver] == 0), 0, jnp.maximum(slack, 0))
    passed = jax.random.randint(jax.random.fold_in(own, 4), (amount // 2,), 0, 1 << 20) % (slack + 1)
    lengths = lengths.at[giver].add(-passed).at[receiver].add(passed)
    items = jnp.searchsorted(jnp.cumsum(lengths), jnp.arange(rows * top), side="right").astype(jnp.int32)
    listing = items.reshape(top, rows).T
    listing = listing[jax.random.permutation(jax.random.fold_in(own, 1), rows)]
    offset_by = jax.random.randint(jax.random.fold_in(own, 2), (rows, 1), 0, top)
    return jnp.take_along_axis(listing, (jnp.arange(top)[None, :] + offset_by) % top, axis=1)


def portions_of(count, total, limit, lean, full):
    weights = [(1 << 20) // math.isqrt(rank ** lean) + 1 for rank in range(1, count + 1)]
    largest = limit if full else min(limit, max(-(-total // count), total * weights[0] // sum(weights)))
    least = 1 if total - largest >= count - 1 else 0
    holding, surplus = [largest] + [least] * (count - 1), total - largest - least * (count - 1)
    while surplus > 0:
        movable = [i for i in range(1, count) if holding[i] < largest] or [i for i in range(1, count) if holding[i] < limit]
        mass, budget = sum([weights[i] for i in movable]), surplus
        for i in movable:
            addition = min(limit - holding[i], max(1, budget * weights[i] // mass), surplus)
            holding[i] = holding[i] + addition
            surplus = surplus - addition
    return np.array(holding)


def bell_draw(rng, extent, scale, most, cuts=(), kind=jnp.bfloat16):
    loudness = block_levels(rng, extent, cuts, -0.22, 0.18) if cuts else 1.0
    array = jax.random.normal(rng, extent, jnp.float32) * scale * loudness
    return jnp.minimum(jnp.maximum(array, -most), most).astype(kind)


def setup_inputs(seed: int = 0) -> dict:
    key_list = jax.random.split(jax.random.key(seed), 14)
    fwd_state = bell_draw(key_list[0], (LAYERS, TOKENS, D), 1.0, 6.0, ((0, 8), (1, 32)))
    new_tokens = bell_draw(key_list[1], (TICKS - 1, TOKENS, D), 1.0, 6.0, ((1, 32),))
    saved_input = bell_draw(key_list[2], (TICKS, LAYERS, TOKENS, D), 1.0, 6.0, ((1, 8), (2, 32)))
    grad_state = bell_draw(key_list[3], (LAYERS, TOKENS, D), 1.0, 6.0, ((0, 8), (1, 32)))
    new_grads = bell_draw(key_list[4], (TICKS - 1, TOKENS, D), 1.0, 6.0, ((1, 32),))
    norm_gain = jnp.clip(1.0 + 0.15 * jax.random.normal(key_list[5], (LAYERS, D), jnp.float32), 0.25, 1.75)
    w_gate = bell_draw(key_list[6], (LAYERS, D, EXPERTS * HID), D ** -0.5, 0.09375, ((0, 8), (2, 32)))
    w_up = bell_draw(key_list[7], (LAYERS, D, EXPERTS * HID), D ** -0.5, 0.09375, ((0, 8), (2, 32)))
    w_down = bell_draw(key_list[8], (LAYERS, EXPERTS * HID, D), HID ** -0.5, 0.1875, ((0, 8), (1, 32)))
    fwd_ids_keys = jax.random.split(jax.random.fold_in(key_list[9], 1), TICKS * LAYERS * TOKENS // TOK_DEV)
    fwd_ids_turns = jax.random.permutation(jax.random.fold_in(key_list[9], 3), TICKS * LAYERS * TOKENS // TOK_DEV)
    fwd_ids = jax.vmap(lambda own, number: assign_block(jax.random.fold_in(key_list[9], 2), own, number, TOK_DEV, EXPERTS, TOPK, CAP, 0))(fwd_ids_keys, fwd_ids_turns).reshape((TICKS, LAYERS, TOKENS, TOPK))
    fwd_gates = jnp.clip(0.05 + 0.55 * jax.random.uniform(key_list[10], (TICKS, LAYERS, TOKENS, TOPK), jnp.float32) ** block_levels(key_list[10], (TICKS, LAYERS, TOKENS, TOPK), ((1, 8), (2, 32)), -0.2, 0.2), 0.05, 0.6)
    bwd_ids_keys = jax.random.split(jax.random.fold_in(key_list[11], 1), TICKS * LAYERS * TOKENS // TOK_DEV)
    bwd_ids_turns = jax.random.permutation(jax.random.fold_in(key_list[11], 3), TICKS * LAYERS * TOKENS // TOK_DEV)
    bwd_ids = jax.vmap(lambda own, number: assign_block(jax.random.fold_in(key_list[11], 2), own, number, TOK_DEV, EXPERTS, TOPK, CAP, 0))(bwd_ids_keys, bwd_ids_turns).reshape((TICKS, LAYERS, TOKENS, TOPK))
    bwd_gates = jnp.clip(0.05 + 0.55 * jax.random.uniform(key_list[12], (TICKS, LAYERS, TOKENS, TOPK), jnp.float32) ** block_levels(key_list[12], (TICKS, LAYERS, TOKENS, TOPK), ((1, 8), (2, 32)), -0.2, 0.2), 0.05, 0.6)
    return {"fwd_state": fwd_state, "new_tokens": new_tokens, "saved_input": saved_input, "grad_state": grad_state, "new_grads": new_grads, "norm_gain": norm_gain, "w_gate": w_gate, "w_up": w_up, "w_down": w_down, "fwd_ids": fwd_ids, "fwd_gates": fwd_gates, "bwd_ids": bwd_ids, "bwd_gates": bwd_gates}


def normalize(activations, gain_row):
    widened = activations.astype(jnp.float32)
    inverse_rms = lax.rsqrt(lax.optimization_barrier(jnp.mean(widened * widened, axis=-1, keepdims=True)) + 1e-06)
    normed = (widened * inverse_rms * gain_row).astype(jnp.bfloat16)
    return (normed, widened, inverse_rms)

def slot_table(route_ids):
    count_rows = route_ids.shape[0] * route_ids.shape[1]
    flat_ids = route_ids.reshape(count_rows).astype(jnp.int32)
    onehot = (flat_ids[:, None] == jnp.arange(EXPERTS, dtype=jnp.int32)[None, :]).astype(jnp.int32)
    blocked = onehot.reshape(N_EXPERT, TOK_DEV * TOPK, EXPERTS)
    rank_table = jnp.cumsum(blocked, axis=1) - 1
    slot_in = lax.optimization_barrier(jnp.sum(rank_table * blocked, axis=2)).reshape(count_rows)
    block_of = jnp.arange(count_rows, dtype=jnp.int32) // (TOK_DEV * TOPK)
    position = (flat_ids * (N_EXPERT * CAP) + block_of * CAP + slot_in).astype(jnp.int32)
    source = jnp.full((EXPERTS * N_EXPERT * CAP,), count_rows, jnp.int32)
    source = source.at[position].set(jnp.arange(count_rows, dtype=jnp.int32))
    return (position, source)

def gather_rows(values, source):
    padded = jnp.concatenate([values, jnp.zeros((1, values.shape[1]), values.dtype)], axis=0)
    return padded[source]

def split_weights(gate_section, up_section, down_section):
    gate_wide = gate_section.astype(jnp.float32).reshape(D, EXPERTS, 2, HID // 2)
    up_wide = up_section.astype(jnp.float32).reshape(D, EXPERTS, 2, HID // 2)
    down_wide = down_section.astype(jnp.float32).reshape(EXPERTS, 2, HID // 2, D)
    return (gate_wide, up_wide, down_wide)

def add_halves(partial_value):
    return (partial_value[:, 0].astype(jnp.float32) + partial_value[:, 1].astype(jnp.float32)).astype(jnp.bfloat16)

def expert_forward(row_block, gate_section, up_section, down_section):
    gate_wide, up_wide, down_wide = split_weights(gate_section, up_section, down_section)
    rows_wide = row_block.astype(jnp.float32)
    gate_pre = jnp.einsum('emd,denh->enmh', rows_wide, gate_wide)
    up_pre = jnp.einsum('emd,denh->enmh', rows_wide, up_wide)
    activated = (jax.nn.silu(gate_pre) * up_pre).astype(jnp.bfloat16)
    partial_value = jnp.einsum('enmh,enhd->enmd', activated.astype(jnp.float32), down_wide).astype(jnp.bfloat16)
    return add_halves(partial_value)

def expert_backward(row_block, grad_block, gate_section, up_section, down_section):
    gate_wide, up_wide, down_wide = split_weights(gate_section, up_section, down_section)
    rows_wide = row_block.astype(jnp.float32)
    grads_wide = grad_block.astype(jnp.float32)
    gate_pre = jnp.einsum('emd,denh->enmh', rows_wide, gate_wide)
    up_pre = jnp.einsum('emd,denh->enmh', rows_wide, up_wide)
    sigmoid_gate = jax.nn.sigmoid(gate_pre)
    silu_value = jax.nn.silu(gate_pre)
    grad_act = jnp.einsum('emd,enhd->enmh', grads_wide, down_wide)
    grad_gate_pre = (grad_act * up_pre * sigmoid_gate * (1.0 + gate_pre * (1.0 - sigmoid_gate))).astype(jnp.bfloat16)
    grad_up_pre = (grad_act * silu_value).astype(jnp.bfloat16)
    partial_value = jnp.einsum('enmh,denh->enmd', grad_gate_pre.astype(jnp.float32), gate_wide)
    partial_value = partial_value + jnp.einsum('enmh,denh->enmd', grad_up_pre.astype(jnp.float32), up_wide)
    return add_halves(partial_value.astype(jnp.bfloat16))

def section_forward(operands):
    activations, gain_row, gate_section, up_section, down_section, route_ids, route_gates = operands
    normed, widened, unused_rms = normalize(activations, gain_row)
    position, source = slot_table(route_ids)
    row_block = gather_rows(normed, source // TOPK).reshape(EXPERTS, N_EXPERT * CAP, D)
    results = expert_forward(row_block, gate_section, up_section, down_section).reshape(EXPERTS * N_EXPERT * CAP, D)
    picked = results[position].astype(jnp.float32).reshape(TOKENS, TOPK, D)
    mixture = lax.optimization_barrier(jnp.sum(picked * route_gates[:, :, None], axis=1))
    return (widened + mixture).astype(jnp.bfloat16)

def section_backward(operands):
    saved, cotangent, gain_row, gate_section, up_section, down_section, route_ids, route_gates = operands
    normed, widened, inverse_rms = normalize(saved, gain_row)
    position, source = slot_table(route_ids)
    row_block = gather_rows(normed, source // TOPK).reshape(EXPERTS, N_EXPERT * CAP, D)
    cot_wide = cotangent.astype(jnp.float32)
    row_grads = (jnp.repeat(cot_wide, TOPK, axis=0) * route_gates.reshape(-1, 1)).astype(jnp.bfloat16)
    grad_block = gather_rows(row_grads, source).reshape(EXPERTS, N_EXPERT * CAP, D)
    grad_rows = expert_backward(row_block, grad_block, gate_section, up_section, down_section)
    returned = grad_rows.reshape(EXPERTS * N_EXPERT * CAP, D)[position].astype(jnp.float32)
    grad_normed = lax.optimization_barrier(jnp.sum(returned.reshape(TOKENS, TOPK, D), axis=1))
    weighted = grad_normed * gain_row
    correction = lax.optimization_barrier(jnp.mean(weighted * widened, axis=-1, keepdims=True))
    grad_input = cot_wide + inverse_rms * weighted - widened * inverse_rms ** 3 * correction
    return grad_input.astype(jnp.bfloat16)

def reference(fwd_state, new_tokens, saved_input, grad_state, new_grads, norm_gain, w_gate, w_up, w_down, fwd_ids, fwd_gates, bwd_ids, bwd_gates):
    current = fwd_state
    cotangent = grad_state
    for step_index in range(TICKS):
        produced = lax.map(section_forward, (current, norm_gain, w_gate, w_up, w_down, fwd_ids[step_index], fwd_gates[step_index]))
        grad_input = lax.map(section_backward, (saved_input[step_index], cotangent, norm_gain, w_gate, w_up, w_down, bwd_ids[step_index], bwd_gates[step_index]))
        if step_index + 1 < TICKS:
            current = jnp.concatenate([new_tokens[step_index][None], produced[:-1]], axis=0)
            cotangent = jnp.concatenate([grad_input[1:], new_grads[step_index][None]], axis=0)
    return (produced, grad_input)
```

```python
import functools

import jax
import jax.numpy as jnp
from jax import lax
from jax.experimental import pallas as pl
from jax.experimental.pallas import tpu as pltpu
from jax.sharding import PartitionSpec as P

MESH = pl.DeviceIdType.MESH
F32 = jnp.float32
BF16 = jnp.bfloat16


def kernel(
    fwd_state,
    new_tokens,
    saved_input,
    grad_state,
    new_grads,
    norm_gain,
    w_gate,
    w_up,
    w_down,
    fwd_ids,
    fwd_gates,
    bwd_ids,
    bwd_gates,
    fwd_out,
    grad_out,
    gate_w,
    up_w,
    down_w,
    send,
    recv,
    partial,
    pair_in,
    back_send,
    back,
    rows_a,
    rows_b,
    gate_pre,
    up_pre,
    grad_act,
    hid_a,
    hid_b,
    stage,
    moved,
    tokens,
    grads,
    weight_sem,
    row_send,
    row_recv,
    swap_send,
    swap_recv,
    pair_send,
    pair_recv,
    back_ssem,
    back_rsem,
    pipe_send,
    pipe_recv,
):
    pipe = lax.axis_index("pipe")
    sections = lax.axis_size("pipe")
    me = lax.axis_index("expert")
    chips = lax.axis_size("expert") // 2
    chip = me // 2
    core = me % 2
    other = chip * 2 + 1 - core
    width = fwd_state.shape[-1]
    token_rows = fwd_state.shape[-2]
    topk = fwd_ids.shape[-1]
    slots = send.shape[2]
    count = chips * slots
    hidden = gate_w.shape[1]
    wide = 512
    after = lax.rem(pipe + 1, sections)
    before = lax.rem(pipe + sections - 1, sections)

    weight_copies = [
        pltpu.make_async_copy(source.at[0], target, weight_sem.at[i])
        for i, (source, target) in enumerate(
            ((w_gate, gate_w), (w_up, up_w), (w_down, down_w))
        )
    ]
    for copy in weight_copies:
        copy.start()

    barrier = pltpu.get_barrier_semaphore()

    @pl.loop(1, chips)
    def _(j):
        peer = lax.rem(chip + j, chips) * 2 + core
        pl.semaphore_signal(barrier, inc=1, device_id={"expert": peer}, device_id_type=MESH)

    pl.semaphore_signal(barrier, inc=1, device_id={"expert": other}, device_id_type=MESH)
    pl.semaphore_signal(barrier, inc=1, device_id={"pipe": after}, device_id_type=MESH)
    pl.semaphore_signal(barrier, inc=1, device_id={"pipe": before}, device_id_type=MESH)

    def columns(i):
        return pl.ds(pl.multiple_of(i * wide, wide), wide)

    def slot_matrix(ids, gates):
        named = lax.broadcasted_iota(jnp.int32, (token_rows, count), 1) // slots
        place = lax.broadcasted_iota(jnp.int32, (token_rows, count), 1) % slots
        chosen = jnp.zeros((token_rows, count), F32)
        weight = jnp.zeros((token_rows, count), F32)
        for k in range(topk):
            hit = ids[:, k : k + 1] == named
            chosen = jnp.where(hit, 1.0, chosen)
            weight = jnp.where(hit, gates[:, k : k + 1], weight)
        row = lax.broadcasted_iota(jnp.int32, (token_rows, token_rows), 0)
        col = lax.broadcasted_iota(jnp.int32, (token_rows, token_rows), 1)
        earlier = jnp.where(col < row, 1.0, 0.0).astype(BF16)
        rank = jnp.dot(earlier, chosen.astype(BF16), preferred_element_type=F32)
        taken = jnp.where(rank == place.astype(F32), chosen, 0.0)
        return taken, taken * weight

    def normalize(values):
        widened = values.astype(F32)
        inverse = lax.rsqrt(jnp.mean(widened * widened, axis=-1, keepdims=True) + 1e-06)
        normed = (widened * inverse * norm_gain[...]).astype(BF16)
        return normed, inverse

    def row_copy(unit, j):
        target = lax.rem(chip + j, chips)
        return pltpu.make_async_remote_copy(
            src_ref=send.at[unit, target],
            dst_ref=recv.at[unit, core, chip],
            send_sem=row_send.at[unit, j],
            recv_sem=row_recv.at[unit, j],
            device_id={"expert": target * 2 + core},
            device_id_type=MESH,
        )

    def row_arrival(unit, j):
        source = lax.rem(chip + chips - j, chips)
        return pltpu.make_async_remote_copy(
            src_ref=send.at[unit, source],
            dst_ref=recv.at[unit, core, source],
            send_sem=row_send.at[unit, j],
            recv_sem=row_recv.at[unit, j],
            device_id={"expert": source * 2 + core},
            device_id_type=MESH,
        )

    def dispatch(unit, source, taken, weighted=None):
        select = jnp.transpose(taken).astype(BF16)
        scale = None
        if weighted is not None:
            scale = jnp.sum(jnp.transpose(weighted), axis=1, keepdims=True)

        @pl.loop(0, width // wide)
        def _(i):
            cut = columns(i)
            rows = jnp.dot(select, source[:, cut], preferred_element_type=F32)
            if scale is not None:
                rows = rows * scale
            send[unit, :, :, cut] = rows.reshape(chips, slots, wide).astype(BF16)

        @pl.loop(1, chips)
        def _(j):
            row_copy(unit, j).start()

        recv[unit, core, chip] = send[unit, chip]

    def swap_copy(unit):
        return pltpu.make_async_remote_copy(
            src_ref=recv.at[unit, core],
            dst_ref=recv.at[unit, core],
            send_sem=swap_send.at[unit],
            recv_sem=swap_recv.at[unit],
            device_id={"expert": other},
            device_id_type=MESH,
        )

    def swap_arrival(unit):
        return pltpu.make_async_remote_copy(
            src_ref=recv.at[unit, 1 - core],
            dst_ref=recv.at[unit, 1 - core],
            send_sem=swap_send.at[unit],
            recv_sem=swap_recv.at[unit],
            device_id={"expert": other},
            device_id_type=MESH,
        )

    def collect(unit):
        @pl.loop(1, chips)
        def _(j):
            row_arrival(unit, j).wait_recv()

        swap_copy(unit).start()

    def gather(unit, target):
        swap_arrival(unit).wait_recv()
        swap_copy(unit).wait_send()

        @pl.loop(0, width // wide)
        def _(i):
            cut = columns(i)
            block = recv[unit, :, :, :, cut].astype(F32)
            target[:, cut] = block.reshape(2 * count, wide).astype(BF16)

    def project():
        @pl.loop(0, hidden // 256)
        def _(i):
            cut = pl.ds(pl.multiple_of(i * 256, 256), 256)
            gate_pre[:, cut] = jnp.dot(rows_a[...], gate_w[:, cut], preferred_element_type=F32)
            up_pre[:, cut] = jnp.dot(rows_a[...], up_w[:, cut], preferred_element_type=F32)

    def split_store(i, values):
        partial[:, :, :, columns(i)] = values.reshape(2, chips, slots, wide).astype(BF16)

    def pair_copy(unit):
        return pltpu.make_async_remote_copy(
            src_ref=partial.at[1 - core],
            dst_ref=pair_in.at[unit],
            send_sem=pair_send.at[unit],
            recv_sem=pair_recv.at[unit],
            device_id={"expert": other},
            device_id_type=MESH,
        )

    def back_copy(unit, j):
        target = lax.rem(chip + j, chips)
        return pltpu.make_async_remote_copy(
            src_ref=back_send.at[unit, target],
            dst_ref=back.at[unit, chip],
            send_sem=back_ssem.at[unit, j],
            recv_sem=back_rsem.at[unit, j],
            device_id={"expert": target * 2 + core},
            device_id_type=MESH,
        )

    def back_arrival(unit, j):
        source = lax.rem(chip + chips - j, chips)
        return pltpu.make_async_remote_copy(
            src_ref=back_send.at[unit, source],
            dst_ref=back.at[unit, source],
            send_sem=back_ssem.at[unit, j],
            recv_sem=back_rsem.at[unit, j],
            device_id={"expert": source * 2 + core},
            device_id_type=MESH,
        )

    def send_back(unit):
        copy = pair_copy(unit)
        copy.start()
        copy.wait()

        @pl.loop(0, width // wide)
        def _(i):
            cut = columns(i)
            both = partial[core, :, :, cut].astype(F32) + pair_in[unit, :, :, cut].astype(F32)
            back_send[unit, :, :, cut] = both.astype(BF16)

        @pl.loop(1, chips)
        def _(j):
            back_copy(unit, j).start()

        back[unit, chip] = back_send[unit, chip]

    def forward(unit):
        project()
        gate = gate_pre[...]
        hid_a[...] = (gate * jax.nn.sigmoid(gate) * up_pre[...]).astype(BF16)

        @pl.loop(0, width // wide)
        def _(i):
            split_store(
                i, jnp.dot(hid_a[...], down_w[:, columns(i)], preferred_element_type=F32)
            )

    def backward(unit):
        project()
        across = (((1,), (1,)), ((), ()))

        @pl.loop(0, hidden // 256)
        def _(i):
            cut = pl.ds(pl.multiple_of(i * 256, 256), 256)
            grad = lax.dot_general(rows_b[...], down_w[cut, :], across, preferred_element_type=F32)
            gate = gate_pre[:, cut]
            sigmoid = jax.nn.sigmoid(gate)
            hid_a[:, cut] = (
                grad * up_pre[:, cut] * sigmoid * (1.0 + gate * (1.0 - sigmoid))
            ).astype(BF16)
            hid_b[:, cut] = (grad * (gate * sigmoid)).astype(BF16)

        @pl.loop(0, width // wide)
        def _(i):
            total = lax.dot_general(
                hid_a[...], gate_w[columns(i), :], across, preferred_element_type=F32
            )
            total = total + lax.dot_general(
                hid_b[...], up_w[columns(i), :], across, preferred_element_type=F32
            )
            split_store(i, total)

    def returned(unit, matrices):
        @pl.loop(1, chips)
        def _(j):
            back_arrival(unit, j).wait_recv()

        @pl.loop(0, width // wide)
        def _(i):
            cut = columns(i)
            rows = back[unit, :, :, cut].astype(F32).reshape(count, wide).astype(BF16)
            total = jnp.zeros((token_rows, wide), F32)
            for matrix in matrices:
                total = total + jnp.dot(matrix, rows, preferred_element_type=F32)
            stage[:, cut] = total

    def mixture(unit, weighted, base, target):
        high = weighted.astype(BF16)
        low = (weighted - high.astype(F32)).astype(BF16)
        returned(unit, (high, low))
        target[...] = (base[...].astype(F32) + stage[...]).astype(BF16)

    def input_grad(unit, taken, saved, inverse, cotangent, target):
        returned(unit, (taken.astype(BF16),))
        weighted = stage[...] * norm_gain[...]
        widened = saved.astype(F32)
        correction = jnp.mean(weighted * widened, axis=-1, keepdims=True)
        target[...] = (
            cotangent[...].astype(F32)
            + inverse * weighted
            - widened * (inverse * inverse * inverse) * correction
        ).astype(BF16)

    def move(which, source, peer):
        return pltpu.make_async_remote_copy(
            src_ref=source,
            dst_ref=moved.at[which],
            send_sem=pipe_send.at[which],
            recv_sem=pipe_recv.at[which],
            device_id={"pipe": peer},
            device_id_type=MESH,
        )

    fwd_slots0 = slot_matrix(fwd_ids[0, 0], fwd_gates[0, 0])
    bwd_slots0 = slot_matrix(bwd_ids[0, 0], bwd_gates[0, 0])
    fwd_slots1 = slot_matrix(fwd_ids[1, 0], fwd_gates[1, 0])
    bwd_slots1 = slot_matrix(bwd_ids[1, 0], bwd_gates[1, 0])
    tokens[...] = normalize(fwd_state[0])[0]

    pl.semaphore_wait(barrier, chips + 2)
    dispatch(0, tokens, fwd_slots0[0])
    normed, inverse0 = normalize(saved_input[0, 0])
    tokens[...] = normed
    dispatch(1, tokens, bwd_slots0[0])
    dispatch(2, grad_state.at[0], *bwd_slots0)
    normed, inverse1 = normalize(saved_input[1, 0])
    tokens[...] = normed

    for copy in weight_copies:
        copy.wait()
    collect(0)
    gather(0, rows_a)
    forward(0)
    send_back(0)

    collect(1)
    collect(2)
    dispatch(3, tokens, bwd_slots1[0])
    gather(1, rows_a)
    gather(2, rows_b)
    backward(1)
    send_back(1)

    mixture(0, fwd_slots0[1], fwd_state.at[0], fwd_out.at[0])
    forth = move(0, fwd_out.at[0], after)
    forth.start()
    forth.wait()
    current = moved.at[0]
    current[...] = jnp.where(pipe == 0, new_tokens[0], current[...])
    tokens[...] = normalize(current[...])[0]
    dispatch(4, tokens, fwd_slots1[0])

    input_grad(1, bwd_slots0[0], saved_input[0, 0], inverse0, grad_state.at[0], grads)
    upward = move(1, grads, before)
    upward.start()
    upward.wait()
    cotangent = moved.at[1]
    cotangent[...] = jnp.where(pipe == sections - 1, new_grads[0], cotangent[...])
    dispatch(5, cotangent, *bwd_slots1)

    collect(3)
    collect(4)
    gather(4, rows_a)
    forward(2)
    send_back(2)

    collect(5)
    gather(3, rows_a)
    gather(5, rows_b)
    backward(3)
    send_back(3)

    mixture(2, fwd_slots1[1], current, fwd_out.at[0])
    input_grad(3, bwd_slots1[0], saved_input[1, 0], inverse1, cotangent, grad_out.at[0])

    for unit in range(6):

        @pl.loop(1, chips)
        def _(j):
            row_copy(unit, j).wait_send()

    for unit in range(4):

        @pl.loop(1, chips)
        def _(j):
            back_copy(unit, j).wait_send()


def shards(*arrays):
    fwd_state, fwd_ids, w_gate = arrays[0], arrays[9], arrays[6]
    token_rows, width = fwd_state.shape[1:]
    hidden = w_gate.shape[2]
    chips = lax.axis_size("expert") // 2
    slots = token_rows * fwd_ids.shape[3] // chips
    count = 2 * chips * slots
    dma = pltpu.SemaphoreType.DMA
    vmem = pl.BlockSpec(memory_space=pltpu.VMEM)
    hbm = pl.BlockSpec(memory_space=pl.ANY)
    row = jax.ShapeDtypeStruct(fwd_state.shape, BF16)
    return pl.pallas_call(
        kernel,
        out_shape=(row, row),
        in_specs=[vmem] * 6 + [hbm] * 3 + [vmem] * 4,
        out_specs=(vmem, vmem),
        scratch_shapes=[
            pltpu.VMEM((width, hidden), BF16),
            pltpu.VMEM((width, hidden), BF16),
            pltpu.VMEM((hidden, width), BF16),
            pltpu.VMEM((6, chips, slots, width), BF16),
            pltpu.VMEM((6, 2, chips, slots, width), BF16),
            pltpu.VMEM((2, chips, slots, width), BF16),
            pltpu.VMEM((4, chips, slots, width), BF16),
            pltpu.VMEM((4, chips, slots, width), BF16),
            pltpu.VMEM((4, chips, slots, width), BF16),
            pltpu.VMEM((count, width), BF16),
            pltpu.VMEM((count, width), BF16),
            pltpu.VMEM((count, hidden), F32),
            pltpu.VMEM((count, hidden), F32),
            pltpu.VMEM((8, 128), F32),
            pltpu.VMEM((count, hidden), BF16),
            pltpu.VMEM((count, hidden), BF16),
            pltpu.VMEM((token_rows, width), F32),
            pltpu.VMEM((2, token_rows, width), BF16),
            pltpu.VMEM((token_rows, width), BF16),
            pltpu.VMEM((token_rows, width), BF16),
            dma((3,)),
            dma((6, chips)),
            dma((6, chips)),
            dma((6,)),
            dma((6,)),
            dma((4,)),
            dma((4,)),
            dma((4, chips)),
            dma((4, chips)),
            dma((2,)),
            dma((2,)),
        ],
        compiler_params=pltpu.CompilerParams(
            collective_id=0, has_side_effects=True, vmem_limit_bytes=60 * 2**20
        ),
        name="relay",
    )(*arrays)


def solution(mesh):
    placed = (
        P("pipe", "expert", None),
        P(None, "expert", None),
        P(None, "pipe", "expert", None),
        P("pipe", "expert", None),
        P(None, "expert", None),
        P("pipe", None),
        P("pipe", None, "expert"),
        P("pipe", None, "expert"),
        P("pipe", "expert", None),
        P(None, "pipe", "expert", None),
        P(None, "pipe", "expert", None),
        P(None, "pipe", "expert", None),
        P(None, "pipe", "expert", None),
    )
    return jax.shard_map(
        shards,
        mesh=mesh,
        in_specs=placed,
        out_specs=(P("pipe", "expert", None), P("pipe", "expert", None)),
        check_vma=False,
    )
```

```python
import functools

import jax
import jax.numpy as jnp
from jax import lax
from jax.experimental import pallas as pl
from jax.experimental.pallas import tpu as pltpu
from jax.sharding import PartitionSpec as P

MESH = pl.DeviceIdType.MESH
F32 = jnp.float32
BF16 = jnp.bfloat16
PARTS = 2
BATCHES = (0, 1, 1, 3, 2, 3)
SCALED = (False, False, True, False, False, True)
LOTS = (0, 1, 2, 3, 0, 2)
FWD_UNITS, ROW_UNITS, GRAD_UNITS = (0, 4), (1, 3), (2, 5)
FAR_ROWS = (
    (0, 7, 0, 1),
    (1, 7, 1, 1),
    (0, 6, 0, 2),
    (0, 5, 0, -1),
    (1, 5, 1, -1),
    (1, 6, 1, -2),
)
FAR_STEPS = ((0, ((0, 1), (1, 1), (0, 2))), (4, ((0, -1), (1, -1), (1, -2))))

ORDER = (
    ("spread", 0),
    ("spread", 1),
    ("tables", 0),
    ("spread", 2),
    ("relay", 0, 0),
    ("relay", 0, 1),
    ("relay", 2, 0),
    ("relay", 1, 1),
    ("relay", 1, 0),
    ("finish", 0, 0),
    ("relay", 2, 1),
    ("finish", 0, 1),
    ("finish", 2, 0),
    ("spread", 3),
    ("finish", 1, 1),
    ("finish", 1, 0),
    ("collect", 0, 0),
    ("finish", 2, 1),
    ("collect", 0, 1),
    ("forward", 0),
    ("back", 0, 0),
    ("collect", 2, 0),
    ("relay", 3, 1),
    ("relay", 3, 0),
    ("collect", 1, 1),
    ("back", 0, 1),
    ("collect", 1, 0),
    ("recompute", 1),
    ("far", 0, 0),
    ("finish", 3, 1),
    ("collect", 2, 1),
    ("finish", 3, 0),
    ("backward", 1),
    ("far", 0, 1),
    ("back", 1, 1),
    ("collect", 3, 1),
    ("near", 0, 0),
    ("near", 0, 1),
    ("collect", 3, 0),
    ("back", 1, 0),
    ("recompute", 3),
    ("far", 1, 1),
    ("own", 0),
    ("far", 1, 0),
    ("near", 1, 1),
    ("near", 1, 0),
    ("spread", 4),
    ("own", 1),
    ("relay", 4, 0),
    ("relay", 4, 1),
    ("finish", 4, 0),
    ("spread", 5),
    ("finish", 4, 1),
    ("relay", 5, 0),
    ("relay", 5, 1),
    ("finish", 5, 0),
    ("collect", 4, 1),
    ("collect", 4, 0),
    ("finish", 5, 1),
    ("forward", 2),
    ("collect", 5, 1),
    ("collect", 5, 0),
    ("back", 2, 0),
    ("back", 2, 1),
    ("backward", 3),
    ("far", 2, 0),
    ("back", 3, 0),
    ("back", 3, 1),
    ("far", 2, 1),
    ("far", 3, 0),
    ("near", 2, 0),
    ("far", 3, 1),
    ("near", 2, 1),
    ("near", 3, 0),
    ("near", 3, 1),
    ("own", 2),
    ("own", 3),
)


def kernel(
    fwd_state,
    new_tokens,
    saved_input,
    grad_state,
    new_grads,
    norm_gain,
    w_gate,
    w_up,
    w_down,
    fwd_ids,
    fwd_gates,
    bwd_ids,
    bwd_gates,
    fwd_out,
    grad_out,
    gate_w,
    up_w,
    down_w,
    meta,
    table,
    held,
    cross,
    far,
    recv,
    partial,
    pair_in,
    results,
    cross_in,
    far_in,
    sums_in,
    sums_out,
    rows_in,
    fwd_gate,
    fwd_up,
    gate_pre,
    up_pre,
    hid_a,
    hid_b,
    stage,
    moved,
    grads,
    weight_sem,
    meta_send,
    meta_recv,
    row_send,
    row_recv,
    swap_send,
    swap_recv,
    pair_send,
    pair_recv,
    back_ssem,
    back_rsem,
    pipe_send,
    pipe_recv,
):
    pipe = lax.axis_index("pipe")
    sections = lax.axis_size("pipe")
    me = lax.axis_index("expert")
    chips = lax.axis_size("expert") // 2
    chip = me // 2
    core = me % 2
    ring = chips // 2
    column = chip // ring
    plane = chip % ring
    other = chip * 2 + 1 - core
    width = fwd_state.shape[-1]
    token_rows = fwd_state.shape[-2]
    topk = fwd_ids.shape[-1]
    slots = recv.shape[4]
    count = chips * slots
    hidden = gate_w.shape[1]
    wide = 256
    after = lax.rem(pipe + 1, sections)
    before = lax.rem(pipe + sections - 1, sections)

    weight_copies = [
        pltpu.make_async_copy(source.at[0], target, weight_sem.at[i])
        for i, (source, target) in enumerate(
            ((w_gate, gate_w), (w_up, up_w), (w_down, down_w))
        )
    ]
    for copy in weight_copies:
        copy.start()

    barrier = pltpu.get_barrier_semaphore()

    @pl.loop(1, chips)
    def _(j):
        peer = lax.rem(chip + j, chips) * 2 + core
        pl.semaphore_signal(barrier, inc=1, device_id={"expert": peer}, device_id_type=MESH)

    pl.semaphore_signal(barrier, inc=1, device_id={"expert": other}, device_id_type=MESH)
    pl.semaphore_signal(barrier, inc=1, device_id={"pipe": after}, device_id_type=MESH)
    pl.semaphore_signal(barrier, inc=1, device_id={"pipe": before}, device_id_type=MESH)

    def columns(i):
        return pl.ds(pl.multiple_of(i * wide, wide), wide)

    def part(half):
        return pl.ds(half * (width // PARTS), width // PARTS)

    def over_part(half):
        steps = width // PARTS // wide
        return pl.loop(half * steps, (half + 1) * steps, unroll=True)

    def device(across, step):
        to_column = lax.rem(column + across, 2)
        to_plane = lax.rem(plane + step + 2 * ring, ring)
        return (to_column * ring + to_plane) * 2 + core

    def expert(across, step):
        return device(across, step) // 2

    def remote(source, target, sends, receives, peer):
        return pltpu.make_async_remote_copy(
            src_ref=source,
            dst_ref=target,
            send_sem=sends,
            recv_sem=receives,
            device_id={"expert": peer},
            device_id_type=MESH,
        )

    def slot_weights(ids, gates):
        named = lax.broadcasted_iota(jnp.int32, (token_rows, count), 1) // slots
        place = lax.broadcasted_iota(jnp.int32, (token_rows, count), 1) % slots
        named = named.astype(F32)
        chosen = jnp.zeros((token_rows, count), F32)
        weight = jnp.zeros((token_rows, count), F32)
        for k in range(topk):
            hit = ids[:, k : k + 1] == named
            chosen = jnp.where(hit, 1.0, chosen)
            weight = jnp.where(hit, gates[:, k : k + 1], weight)
        row = lax.broadcasted_iota(jnp.int32, (token_rows, token_rows), 0)
        col = lax.broadcasted_iota(jnp.int32, (token_rows, token_rows), 1)
        earlier = jnp.where(col < row, 1.0, 0.0).astype(BF16)
        rank = jnp.dot(earlier, chosen.astype(BF16), preferred_element_type=F32)
        return jnp.where(rank == place.astype(F32), weight, 0.0)

    def inverse_rms(widened):
        return lax.rsqrt(jnp.mean(widened * widened, axis=-1, keepdims=True) + 1e-06)

    def normalize(values):
        widened = values.astype(F32)
        return (widened * inverse_rms(widened) * norm_gain[...]).astype(BF16)

    meta_copies = [
        remote(meta.at[2], meta.at[2 - step], meta_send.at[i], meta_recv.at[i], device(0, step))
        for i, step in enumerate((1, -1, 2, -2))
    ]

    def first_hop(unit, half):
        return [
            remote(
                held.at[unit, 2, :, part(half)],
                held.at[unit, 2 - step, :, part(half)],
                row_send.at[unit, half, i],
                row_recv.at[unit, half, i],
                device(0, step),
            )
            for i, step in enumerate((1, -1))
        ]

    def second_hop(unit, half):
        return [
            remote(
                held.at[unit, 2 - step, :, part(half)],
                held.at[unit, 2 - 2 * step, :, part(half)],
                row_send.at[unit, half, 2 + i],
                row_recv.at[unit, half, 2 + i],
                device(0, step),
            )
            for i, step in enumerate((1, -1))
        ]

    def cross_copies(unit, half):
        return [
            remote(
                cross.at[LOTS[unit], slots_of, :, part(half)],
                recv.at[unit, core, 1, slots_of, :, part(half)],
                row_send.at[unit, half, 4 + i],
                row_recv.at[unit, half, 4 + i],
                device(1, 0),
            )
            for i, slots_of in enumerate((pl.ds(1, 3), pl.ds(0, 1), pl.ds(4, 1)))
        ]

    def far_copies(unit, half):
        return [
            remote(
                far.at[LOTS[unit], i, :, part(half)],
                recv.at[unit, core, to, slot, :, part(half)],
                row_send.at[unit, half, 7 + i],
                row_recv.at[unit, half, 7 + i],
                device(across, step),
            )
            for i, (to, slot, across, step) in enumerate(FAR_ROWS)
        ]

    def pick(unit, half, first, many, targets):
        share = len(targets) // many
        batch, scaled = BATCHES[unit], SCALED[unit]
        picked = jnp.concatenate(
            [table[batch, first + n // share, e] for n, (e, _) in enumerate(targets)], axis=0
        )
        scale = jnp.sum(picked, axis=1, keepdims=True)
        if many > 1:
            picked = jnp.concatenate([picked] * many, axis=1)
            row = lax.broadcasted_iota(jnp.int32, picked.shape, 0) // (share * slots)
            col = lax.broadcasted_iota(jnp.int32, picked.shape, 1) // token_rows
            picked = jnp.where(row == col, picked, 0.0)
        select = jnp.where(picked > 0.0, 1.0, 0.0).astype(BF16)

        @over_part(half)
        def _(i):
            cut = columns(i)
            block = held[unit, pl.ds(first, many), :, cut].reshape(many * token_rows, wide)
            rows = jnp.dot(select, block, preferred_element_type=F32)
            if scaled:
                rows = rows * scale
            for n, (_, target) in enumerate(targets):
                target[:, cut] = rows[n * slots : (n + 1) * slots].astype(BF16)

    def near(unit, slot):
        return [
            (expert(0, 0), recv.at[unit, core, 0, slot]),
            (expert(1, 0), cross.at[LOTS[unit], slot]),
        ]

    def spread(unit):
        for half in range(PARTS):
            for copy in first_hop(unit, half):
                copy.start()

    def relay(unit, half):
        arrivals, onward = first_hop(unit, half), second_hop(unit, half)
        for i in range(2):
            arrivals[i].wait_recv()
            onward[i].start()
        targets = [target for slot in (1, 2, 3) for target in near(unit, slot)]
        pick(unit, half, 1, 3, targets)
        cross_copies(unit, half)[0].start()

    def finish(unit, half):
        arrivals, beyond = second_hop(unit, half), far_copies(unit, half)
        crossing = cross_copies(unit, half)
        for i, (slot, steps) in enumerate(FAR_STEPS):
            arrivals[i].wait_recv()
            targets = near(unit, slot) + [
                (expert(*at), far.at[LOTS[unit], 3 * i + n]) for n, at in enumerate(steps)
            ]
            pick(unit, half, slot, 1, targets)
            for n in range(3):
                beyond[3 * i + n].start()
            crossing[1 + i].start()

    def release(unit):
        for half in range(PARTS):
            for copy in cross_copies(unit, half) + far_copies(unit, half):
                copy.wait_send()

    def swap_copy(unit, half, rail):
        half_rows = recv.at[unit, rail, :, :, :, part(half)]
        return remote(
            half_rows, half_rows, swap_send.at[unit, half], swap_recv.at[unit, half], other
        )

    def collect(unit, half):
        for copy in cross_copies(unit, half) + far_copies(unit, half):
            copy.wait_recv()
        swap_copy(unit, half, core).start()

    def gather(unit):
        for half in range(PARTS):
            swap_copy(unit, half, 1 - core).wait_recv()
            swap_copy(unit, half, core).wait_send()

            @over_part(half)
            def _(i):
                cut = columns(i)
                block = recv[unit, :, :, :, :, cut].astype(F32)
                rows_in[:, cut] = block.reshape(2 * count, wide).astype(BF16)

    def project(gate_to, up_to):
        @pl.loop(0, hidden // 256)
        def _(i):
            cut = pl.ds(pl.multiple_of(i * 256, 256), 256)
            gate_to[:, cut] = jnp.dot(rows_in[...], gate_w[:, cut], preferred_element_type=F32)
            up_to[:, cut] = jnp.dot(rows_in[...], up_w[:, cut], preferred_element_type=F32)

    def pair_copy(unit, half):
        return remote(
            partial.at[unit % 2, 1 - core, :, :, :, part(half)],
            pair_in.at[unit, :, :, :, part(half)],
            pair_send.at[unit, half],
            pair_recv.at[unit, half],
            other,
        )

    def result_copies(unit, half):
        crossing = remote(
            results.at[unit, 1, pl.ds(0, 5), :, part(half)],
            cross_in.at[unit, :, :, part(half)],
            back_ssem.at[unit, half, 0],
            back_rsem.at[unit, half, 0],
            device(1, 0),
        )
        return [crossing] + [
            remote(
                results.at[unit, to, slot, :, part(half)],
                far_in.at[unit, i, :, part(half)],
                back_ssem.at[unit, half, 1 + i],
                back_rsem.at[unit, half, 1 + i],
                device(across, -step),
            )
            for i, (to, slot, across, step) in enumerate(FAR_ROWS)
        ]

    def sum_copies(unit, half, hop):
        return [
            remote(
                sums_out.at[unit % 2, hop, i, :, part(half)],
                sums_in.at[unit, hop, i, :, part(half)],
                back_ssem.at[unit, half, 7 + 2 * hop + i],
                back_rsem.at[unit, half, 7 + 2 * hop + i],
                device(0, step),
            )
            for i, step in enumerate((-1, 1))
        ]

    def combine(unit, half, slot, terms, added, put):
        gated = unit % 2 == 0
        weights = jnp.transpose(
            jnp.concatenate([table[unit, slot, e] for e, _ in terms], axis=0)
        )
        if gated:
            high = weights.astype(BF16)
            low = (weights - high.astype(F32)).astype(BF16)
            matrix = jnp.concatenate([high, low], axis=0)
        else:
            matrix = jnp.where(weights > 0.0, 1.0, 0.0).astype(BF16)

        @over_part(half)
        def _(i):
            cut = columns(i)
            rows = jnp.concatenate([term[:, cut].astype(F32) for _, term in terms], axis=0)
            total = jnp.dot(matrix, rows.astype(BF16), preferred_element_type=F32)
            if gated:
                total = total[:token_rows] + total[token_rows:]
            for extra in added:
                total = total + extra[:, cut].astype(F32)
            put(cut, total)

    def close_terms(unit, slot):
        return [
            (expert(0, 0), results.at[unit, 0, slot]),
            (expert(1, 0), cross_in.at[unit, slot]),
        ]

    def sum_far(unit, half):
        onward = sum_copies(unit, half, 0)
        for copy in result_copies(unit, half):
            copy.wait_recv()
        for i, (slot, steps) in enumerate(FAR_STEPS):
            terms = close_terms(unit, slot) + [
                (expert(*at), far_in.at[unit, 3 * i + n]) for n, at in enumerate(steps)
            ]
            target = sums_out.at[unit % 2, 0, i]

            def put(cut, total):
                target[:, cut] = total.astype(BF16)

            combine(unit, half, slot, terms, [], put)
            onward[i].start()

    def sum_near(unit, half):
        arrivals, onward = sum_copies(unit, half, 0), sum_copies(unit, half, 1)
        for i, slot in enumerate((1, 3)):
            arrivals[i].wait_recv()
            target = sums_out.at[unit % 2, 1, i]

            def put(cut, total):
                target[:, cut] = total.astype(BF16)

            terms = close_terms(unit, slot)
            combine(unit, half, slot, terms, [sums_in.at[unit, 0, i]], put)
            onward[i].start()

    def sum_own(unit):
        def put(cut, total):
            stage[:, cut] = total

        added = [sums_in.at[unit, 1, i] for i in range(2)]
        for half in range(PARTS):
            for copy in sum_copies(unit, half, 1):
                copy.wait_recv()
            combine(unit, half, 2, close_terms(unit, 2), added, put)

    def sums_sent(unit):
        for half in range(PARTS):
            for hop in range(2):
                for copy in sum_copies(unit, half, hop):
                    copy.wait_send()

    def send_back(unit, half):
        pair_copy(unit, half).wait()

        @over_part(half)
        def _(i):
            cut = columns(i)
            mine = partial[unit % 2, core, :, :, :, cut].astype(F32)
            both = mine + pair_in[unit, :, :, :, cut].astype(F32)
            results[unit, :, :, :, cut] = both.astype(BF16)

        for copy in result_copies(unit, half):
            copy.start()

    def outputs(unit, rows):
        for half in range(PARTS):

            @over_part(half)
            def _(i):
                values = rows(columns(i)).reshape(2, 2, ring, slots, wide)
                partial[unit % 2, :, :, :, :, columns(i)] = values.astype(BF16)

            pair_copy(unit, half).start()

    def forward(unit):
        gather(FWD_UNITS[unit // 2])
        project(fwd_gate, fwd_up)
        gate = fwd_gate[...]
        hid_a[...] = (gate * jax.nn.sigmoid(gate) * fwd_up[...]).astype(BF16)
        outputs(
            unit, lambda cut: jnp.dot(hid_a[...], down_w[:, cut], preferred_element_type=F32)
        )

    def recompute(unit):
        gather(ROW_UNITS[unit // 2])
        project(gate_pre, up_pre)

    def backward(unit):
        gather(GRAD_UNITS[unit // 2])
        across = (((1,), (1,)), ((), ()))

        @pl.loop(0, hidden // 256)
        def _(i):
            cut = pl.ds(pl.multiple_of(i * 256, 256), 256)
            grad = lax.dot_general(rows_in[...], down_w[cut, :], across, preferred_element_type=F32)
            gate = gate_pre[:, cut]
            sigmoid = jax.nn.sigmoid(gate)
            hid_a[:, cut] = (
                grad * up_pre[:, cut] * sigmoid * (1.0 + gate * (1.0 - sigmoid))
            ).astype(BF16)
            hid_b[:, cut] = (grad * (gate * sigmoid)).astype(BF16)

        def rows(cut):
            total = lax.dot_general(
                hid_a[...], gate_w[cut, :], across, preferred_element_type=F32
            )
            return total + lax.dot_general(
                hid_b[...], up_w[cut, :], across, preferred_element_type=F32
            )

        outputs(unit, rows)

    def mixture(unit, base, target):
        sum_own(unit)
        target[...] = (base[...].astype(F32) + stage[...]).astype(BF16)

    def input_grad(unit, saved, cotangent, target):
        sum_own(unit)
        weighted = stage[...] * norm_gain[...]
        widened = saved.astype(F32)
        inverse = inverse_rms(widened)
        correction = jnp.mean(weighted * widened, axis=-1, keepdims=True)
        target[...] = (
            cotangent[...].astype(F32)
            + inverse * weighted
            - widened * (inverse * inverse * inverse) * correction
        ).astype(BF16)

    def move(which, source, peer):
        return pltpu.make_async_remote_copy(
            src_ref=source,
            dst_ref=moved.at[which],
            send_sem=pipe_send.at[which],
            recv_sem=pipe_recv.at[which],
            device_id={"pipe": peer},
            device_id_type=MESH,
        )

    for batch, (ids, gates) in enumerate(
        ((fwd_ids, fwd_gates), (bwd_ids, bwd_gates), (fwd_ids, fwd_gates), (bwd_ids, bwd_gates))
    ):
        begin = 2 * topk * batch
        meta[2, :, begin : begin + topk] = ids[batch // 2, 0].astype(F32)
        meta[2, :, begin + topk : begin + 2 * topk] = gates[batch // 2, 0]
    current, cotangent = moved.at[0], moved.at[1]
    forth = move(0, fwd_out.at[0], after)
    upward = move(1, grads, before)

    def begin_spread(unit):
        if unit == 0:
            held[0, 2] = normalize(fwd_state[0])
            pl.semaphore_wait(barrier, chips + 2)
            for copy in meta_copies:
                copy.start()
        elif unit == 1:
            held[1, 2] = normalize(saved_input[0, 0])
        elif unit == 2:
            held[2, 2] = grad_state[0]
        elif unit == 3:
            held[3, 2] = normalize(saved_input[1, 0])
        elif unit == 4:
            forth.wait()
            current[...] = jnp.where(pipe == 0, new_tokens[0], current[...])
            held[4, 2] = normalize(current[...])
            release(0)
            sums_sent(0)
        else:
            upward.wait()
            cotangent[...] = jnp.where(pipe == sections - 1, new_grads[0], cotangent[...])
            held[5, 2] = cotangent[...]
            release(2)
            sums_sent(1)
        spread(unit)

    def tables(_):
        for copy in meta_copies:
            copy.wait_recv()

        @pl.loop(0, 5)
        def _(slot):
            for batch in range(4):
                begin = 2 * topk * batch
                weights = slot_weights(
                    meta[slot, :, begin : begin + topk],
                    meta[slot, :, begin + topk : begin + 2 * topk],
                )
                table[batch, slot] = jnp.transpose(weights).reshape(chips, slots, token_rows)

        for copy in weight_copies:
            copy.wait()

    def complete(unit):
        if unit == 0:
            mixture(0, fwd_state.at[0], fwd_out.at[0])
            forth.start()
        elif unit == 1:
            input_grad(1, saved_input[0, 0], grad_state.at[0], grads)
            upward.start()
        elif unit == 2:
            mixture(2, current, fwd_out.at[0])
        else:
            input_grad(3, saved_input[1, 0], cotangent, grad_out.at[0])

    steps = {
        "spread": begin_spread,
        "tables": tables,
        "relay": relay,
        "finish": finish,
        "collect": collect,
        "forward": forward,
        "recompute": recompute,
        "backward": backward,
        "back": send_back,
        "far": sum_far,
        "near": sum_near,
        "own": complete,
    }
    for name, *which in ORDER:
        steps[name](*which)

    for copy in meta_copies:
        copy.wait_send()
    for unit in range(6):
        for half in range(PARTS):
            for copy in first_hop(unit, half) + second_hop(unit, half):
                copy.wait_send()
    for unit in (4, 1, 5, 3):
        release(unit)
    for unit in (2, 3):
        sums_sent(unit)
    for unit in range(4):
        for half in range(PARTS):
            for copy in result_copies(unit, half):
                copy.wait_send()


def shards(*arrays):
    fwd_state, fwd_ids, w_gate = arrays[0], arrays[9], arrays[6]
    token_rows, width = fwd_state.shape[1:]
    hidden = w_gate.shape[2]
    chips = lax.axis_size("expert") // 2
    slots = token_rows * fwd_ids.shape[3] // chips
    count = 2 * chips * slots
    dma = pltpu.SemaphoreType.DMA
    vmem = pl.BlockSpec(memory_space=pltpu.VMEM)
    hbm = pl.BlockSpec(memory_space=pl.ANY)
    row = jax.ShapeDtypeStruct(fwd_state.shape, BF16)
    return pl.pallas_call(
        kernel,
        out_shape=(row, row),
        in_specs=[vmem] * 6 + [hbm] * 3 + [vmem] * 4,
        out_specs=(vmem, vmem),
        scratch_shapes=[
            pltpu.VMEM((width, hidden), BF16),
            pltpu.VMEM((width, hidden), BF16),
            pltpu.VMEM((hidden, width), BF16),
            pltpu.VMEM((5, token_rows, 128), F32),
            pltpu.VMEM((4, 5, chips, slots, token_rows), F32),
            pltpu.VMEM((6, 5, token_rows, width), BF16),
            pltpu.VMEM((4, 5, slots, width), BF16),
            pltpu.VMEM((4, 6, slots, width), BF16),
            pltpu.VMEM((6, 2, 2, chips // 2, slots, width), BF16),
            pltpu.VMEM((2, 2, 2, chips // 2, slots, width), BF16),
            pltpu.VMEM((4, 2, chips // 2, slots, width), BF16),
            pltpu.VMEM((4, 2, chips // 2, slots, width), BF16),
            pltpu.VMEM((4, 5, slots, width), BF16),
            pltpu.VMEM((4, 6, slots, width), BF16),
            pltpu.VMEM((4, 2, 2, token_rows, width), BF16),
            pltpu.VMEM((2, 2, 2, token_rows, width), BF16),
            pltpu.VMEM((count, width), BF16),
            pltpu.VMEM((count, hidden), F32),
            pltpu.VMEM((count, hidden), F32),
            pltpu.VMEM((count, hidden), F32),
            pltpu.VMEM((count, hidden), F32),
            pltpu.VMEM((count, hidden), BF16),
            pltpu.VMEM((count, hidden), BF16),
            pltpu.VMEM((token_rows, width), F32),
            pltpu.VMEM((2, token_rows, width), BF16),
            pltpu.VMEM((token_rows, width), BF16),
            dma((3,)),
            dma((4,)),
            dma((4,)),
            dma((6, PARTS, 13)),
            dma((6, PARTS, 13)),
            dma((6, PARTS)),
            dma((6, PARTS)),
            dma((4, PARTS)),
            dma((4, PARTS)),
            dma((4, PARTS, 11)),
            dma((4, PARTS, 11)),
            dma((2,)),
            dma((2,)),
        ],
        compiler_params=pltpu.CompilerParams(
            collective_id=0, has_side_effects=True, vmem_limit_bytes=60 * 2**20
        ),
        name="relay",
    )(*arrays)


def solution(mesh):
    placed = (
        P("pipe", "expert", None),
        P(None, "expert", None),
        P(None, "pipe", "expert", None),
        P("pipe", "expert", None),
        P(None, "expert", None),
        P("pipe", None),
        P("pipe", None, "expert"),
        P("pipe", None, "expert"),
        P("pipe", "expert", None),
        P(None, "pipe", "expert", None),
        P(None, "pipe", "expert", None),
        P(None, "pipe", "expert", None),
        P(None, "pipe", "expert", None),
    )
    return jax.shard_map(
        shards,
        mesh=mesh,
        in_specs=placed,
        out_specs=(P("pipe", "expert", None), P("pipe", "expert", None)),
        check_vma=False,
    )
```

```python
import functools

import jax
import jax.numpy as jnp
from jax import lax
from jax.experimental import pallas as pl
from jax.experimental.pallas import tpu as pltpu
from jax.sharding import PartitionSpec as P

MESH = pl.DeviceIdType.MESH
F32 = jnp.float32
BF16 = jnp.bfloat16
PARTS = 2
BATCHES = (0, 1, 1, 3, 2, 3)
SCALED = (False, False, True, False, False, True)
LOTS = (0, 1, 2, 3, 0, 2)
FWD_UNITS, ROW_UNITS, GRAD_UNITS = (0, 4), (1, 3), (2, 5)
FAR_ROWS = (
    (0, 7, 0, 1),
    (1, 7, 1, 1),
    (0, 6, 0, 2),
    (0, 5, 0, -1),
    (1, 5, 1, -1),
    (1, 6, 1, -2),
)
FAR_STEPS = ((0, ((0, 1), (1, 1), (0, 2))), (4, ((0, -1), (1, -1), (1, -2))))

ORDER = (
    ("spread", 2),
    ("spread", 1),
    ("spread", 0),
    ("tables", 0),
    ("relay", 2, 0),
    ("relay", 2, 1),
    ("relay", 1, 0),
    ("relay", 1, 1),
    ("finish", 2, 0),
    ("finish", 1, 0),
    ("finish", 1, 1),
    ("finish", 2, 1),
    ("relay", 0, 0),
    ("relay", 0, 1),
    ("spread", 3),
    ("collect", 2, 0),
    ("collect", 1, 0),
    ("collect", 1, 1),
    ("recompute", 1),
    ("collect", 2, 1),
    ("finish", 0, 0),
    ("finish", 0, 1),
    ("backward", 1),
    ("relay", 3, 0),
    ("back", 1, 0),
    ("back", 1, 1),
    ("collect", 0, 0),
    ("collect", 0, 1),
    ("finish", 3, 0),
    ("forward", 0),
    ("far", 1, 0),
    ("back", 0, 1),
    ("far", 1, 1),
    ("back", 0, 0),
    ("collect", 3, 0),
    ("near", 1, 0),
    ("near", 1, 1),
    ("far", 0, 1),
    ("far", 0, 0),
    ("own", 1),
    ("relay", 3, 1),
    ("near", 0, 1),
    ("near", 0, 0),
    ("spread", 5),
    ("finish", 3, 1),
    ("own", 0),
    ("relay", 5, 0),
    ("relay", 5, 1),
    ("spread", 4),
    ("finish", 5, 0),
    ("relay", 4, 0),
    ("finish", 5, 1),
    ("collect", 3, 1),
    ("recompute", 3),
    ("relay", 4, 1),
    ("collect", 5, 0),
    ("finish", 4, 0),
    ("collect", 5, 1),
    ("finish", 4, 1),
    ("backward", 3),
    ("back", 3, 0),
    ("collect", 4, 1),
    ("collect", 4, 0),
    ("back", 3, 1),
    ("forward", 2),
    ("far", 3, 0),
    ("back", 2, 0),
    ("back", 2, 1),
    ("near", 3, 0),
    ("far", 3, 1),
    ("far", 2, 0),
    ("far", 2, 1),
    ("near", 3, 1),
    ("near", 2, 0),
    ("near", 2, 1),
    ("own", 3),
    ("own", 2),
)


def kernel(
    fwd_state,
    new_tokens,
    saved_input,
    grad_state,
    new_grads,
    norm_gain,
    w_gate,
    w_up,
    w_down,
    fwd_ids,
    fwd_gates,
    bwd_ids,
    bwd_gates,
    fwd_out,
    grad_out,
    inputs,
    gain,
    ids,
    gates,
    outs,
    input_sem,
    output_sem,
    gate_w,
    up_w,
    down_w,
    meta,
    table,
    held,
    cross,
    far,
    recv,
    partial,
    pair_in,
    results,
    cross_in,
    far_in,
    sums_in,
    sums_out,
    rows_in,
    fwd_gate,
    fwd_up,
    gate_pre,
    up_pre,
    hid_a,
    hid_b,
    stage,
    moved,
    grads,
    meta_send,
    meta_recv,
    row_send,
    row_recv,
    swap_send,
    swap_recv,
    pair_send,
    pair_recv,
    back_ssem,
    back_rsem,
    pipe_send,
    pipe_recv,
):
    pipe = lax.axis_index("pipe")
    sections = lax.axis_size("pipe")
    me = lax.axis_index("expert")
    chips = lax.axis_size("expert") // 2
    chip = me // 2
    core = me % 2
    ring = chips // 2
    column = chip // ring
    plane = chip % ring
    other = chip * 2 + 1 - core
    width = fwd_state.shape[-1]
    token_rows = fwd_state.shape[-2]
    topk = fwd_ids.shape[-2]
    slots = recv.shape[4]
    count = chips * slots
    hidden = gate_w.shape[1]
    wide = 256
    after = lax.rem(pipe + 1, sections)
    before = lax.rem(pipe + sections - 1, sections)

    barrier = pltpu.get_barrier_semaphore()

    @pl.loop(1, chips)
    def _(j):
        peer = lax.rem(chip + j, chips) * 2 + core
        pl.semaphore_signal(barrier, inc=1, device_id={"expert": peer}, device_id_type=MESH)

    pl.semaphore_signal(barrier, inc=1, device_id={"expert": other}, device_id_type=MESH)
    pl.semaphore_signal(barrier, inc=1, device_id={"pipe": after}, device_id_type=MESH)
    pl.semaphore_signal(barrier, inc=1, device_id={"pipe": before}, device_id_type=MESH)

    sources = {
        "fwd_ids": (fwd_ids.at[:, 0], ids.at[0]),
        "fwd_gates": (fwd_gates.at[:, 0], gates.at[0]),
        "bwd_ids": (bwd_ids.at[:, 0], ids.at[1]),
        "bwd_gates": (bwd_gates.at[:, 0], gates.at[1]),
        "grad_state": (grad_state.at[0], held.at[2, 2]),
        "gain": (norm_gain, gain),
        "saved0": (saved_input.at[0, 0], inputs.at[2]),
        "fwd_state": (fwd_state.at[0], inputs.at[0]),
        "saved1": (saved_input.at[1, 0], inputs.at[3]),
        "gate": (w_gate.at[0], gate_w),
        "up": (w_up.at[0], up_w),
        "down": (w_down.at[0], down_w),
        "new_tokens": (new_tokens.at[0], inputs.at[1]),
        "new_grads": (new_grads.at[0], inputs.at[4]),
    }
    loads = {
        key: pltpu.make_async_copy(source, target, input_sem.at[i])
        for i, (key, (source, target)) in enumerate(sources.items())
    }
    for load in loads.values():
        load.start()

    def need(*keys):
        for key in keys:
            if key in loads:
                loads.pop(key).wait()

    def columns(i):
        return pl.ds(pl.multiple_of(i * wide, wide), wide)

    def part(half):
        return pl.ds(half * (width // PARTS), width // PARTS)

    def over_part(half):
        steps = width // PARTS // wide
        return pl.loop(half * steps, (half + 1) * steps, unroll=True)

    def device(across, step):
        to_column = lax.rem(column + across, 2)
        to_plane = lax.rem(plane + step + 2 * ring, ring)
        return (to_column * ring + to_plane) * 2 + core

    def expert(across, step):
        return device(across, step) // 2

    def remote(source, target, sends, receives, peer):
        return pltpu.make_async_remote_copy(
            src_ref=source,
            dst_ref=target,
            send_sem=sends,
            recv_sem=receives,
            device_id={"expert": peer},
            device_id_type=MESH,
        )

    def slot_weights(ids, gates):
        named = lax.broadcasted_iota(jnp.int32, (count, token_rows), 0) // slots
        place = lax.broadcasted_iota(jnp.int32, (count, token_rows), 0) % slots
        named = named.astype(F32)
        chosen = jnp.zeros((count, token_rows), F32)
        weight = jnp.zeros((count, token_rows), F32)
        for k in range(topk):
            hit = ids[k : k + 1] == named
            chosen = jnp.where(hit, 1.0, chosen)
            weight = jnp.where(hit, gates[k : k + 1], weight)
        row = lax.broadcasted_iota(jnp.int32, (token_rows, token_rows), 0)
        col = lax.broadcasted_iota(jnp.int32, (token_rows, token_rows), 1)
        earlier = jnp.where(row < col, 1.0, 0.0).astype(BF16)
        rank = jnp.dot(chosen.astype(BF16), earlier, preferred_element_type=F32)
        return jnp.where(rank == place.astype(F32), weight, 0.0)

    def inverse_rms(widened):
        return lax.rsqrt(jnp.mean(widened * widened, axis=-1, keepdims=True) + 1e-06)

    def normalize(values):
        widened = values.astype(F32)
        return (widened * inverse_rms(widened) * gain[...]).astype(BF16)

    meta_copies = [
        remote(meta.at[2], meta.at[2 - step], meta_send.at[i], meta_recv.at[i], device(0, step))
        for i, step in enumerate((1, -1, 2, -2))
    ]

    def first_hop(unit, half):
        return [
            remote(
                held.at[unit, 2, :, part(half)],
                held.at[unit, 2 - step, :, part(half)],
                row_send.at[unit, half, i],
                row_recv.at[unit, half, i],
                device(0, step),
            )
            for i, step in enumerate((1, -1))
        ]

    def second_hop(unit, half):
        return [
            remote(
                held.at[unit, 2 - step, :, part(half)],
                held.at[unit, 2 - 2 * step, :, part(half)],
                row_send.at[unit, half, 2 + i],
                row_recv.at[unit, half, 2 + i],
                device(0, step),
            )
            for i, step in enumerate((1, -1))
        ]

    def cross_copies(unit, half):
        return [
            remote(
                cross.at[LOTS[unit], slots_of, :, part(half)],
                recv.at[unit, core, 1, slots_of, :, part(half)],
                row_send.at[unit, half, 4 + i],
                row_recv.at[unit, half, 4 + i],
                device(1, 0),
            )
            for i, slots_of in enumerate((pl.ds(1, 3), pl.ds(0, 1), pl.ds(4, 1)))
        ]

    def far_copies(unit, half):
        return [
            remote(
                far.at[LOTS[unit], i, :, part(half)],
                recv.at[unit, core, to, slot, :, part(half)],
                row_send.at[unit, half, 7 + i],
                row_recv.at[unit, half, 7 + i],
                device(across, step),
            )
            for i, (to, slot, across, step) in enumerate(FAR_ROWS)
        ]

    def pick(unit, half, first, many, targets):
        share = len(targets) // many
        batch, scaled = BATCHES[unit], SCALED[unit]
        picked = jnp.concatenate(
            [table[batch, first + n // share, e] for n, (e, _) in enumerate(targets)], axis=0
        )
        scale = jnp.sum(picked, axis=1, keepdims=True)
        if many > 1:
            picked = jnp.concatenate([picked] * many, axis=1)
            row = lax.broadcasted_iota(jnp.int32, picked.shape, 0) // (share * slots)
            col = lax.broadcasted_iota(jnp.int32, picked.shape, 1) // token_rows
            picked = jnp.where(row == col, picked, 0.0)
        select = jnp.where(picked > 0.0, 1.0, 0.0).astype(BF16)

        @over_part(half)
        def _(i):
            cut = columns(i)
            block = held[unit, pl.ds(first, many), :, cut].reshape(many * token_rows, wide)
            rows = jnp.dot(select, block, preferred_element_type=F32)
            if scaled:
                rows = rows * scale
            for n, (_, target) in enumerate(targets):
                target[:, cut] = rows[n * slots : (n + 1) * slots].astype(BF16)

    def near(unit, slot):
        return [
            (expert(0, 0), recv.at[unit, core, 0, slot]),
            (expert(1, 0), cross.at[LOTS[unit], slot]),
        ]

    def spread(unit):
        for half in range(PARTS):
            for copy in first_hop(unit, half):
                copy.start()

    def relay(unit, half):
        arrivals, onward = first_hop(unit, half), second_hop(unit, half)
        for i in range(2):
            arrivals[i].wait_recv()
            onward[i].start()
        targets = [target for slot in (1, 2, 3) for target in near(unit, slot)]
        pick(unit, half, 1, 3, targets)
        cross_copies(unit, half)[0].start()

    def finish(unit, half):
        arrivals, beyond = second_hop(unit, half), far_copies(unit, half)
        crossing = cross_copies(unit, half)
        for i, (slot, steps) in enumerate(FAR_STEPS):
            arrivals[i].wait_recv()
            targets = near(unit, slot) + [
                (expert(*at), far.at[LOTS[unit], 3 * i + n]) for n, at in enumerate(steps)
            ]
            pick(unit, half, slot, 1, targets)
            for n in range(3):
                beyond[3 * i + n].start()
            crossing[1 + i].start()

    def release(unit):
        for half in range(PARTS):
            for copy in cross_copies(unit, half) + far_copies(unit, half):
                copy.wait_send()

    def swap_copy(unit, half, rail):
        half_rows = recv.at[unit, rail, :, :, :, part(half)]
        return remote(
            half_rows, half_rows, swap_send.at[unit, half], swap_recv.at[unit, half], other
        )

    def collect(unit, half):
        for copy in cross_copies(unit, half) + far_copies(unit, half):
            copy.wait_recv()
        swap_copy(unit, half, core).start()

    def gather(unit):
        for half in range(PARTS):
            swap_copy(unit, half, 1 - core).wait_recv()
            swap_copy(unit, half, core).wait_send()

            @over_part(half)
            def _(i):
                cut = columns(i)
                block = recv[unit, :, :, :, :, cut].astype(F32)
                rows_in[:, cut] = block.reshape(2 * count, wide).astype(BF16)

    def project(gate_to, up_to):
        @pl.loop(0, hidden // 256)
        def _(i):
            cut = pl.ds(pl.multiple_of(i * 256, 256), 256)
            gate_to[:, cut] = jnp.dot(rows_in[...], gate_w[:, cut], preferred_element_type=F32)
            up_to[:, cut] = jnp.dot(rows_in[...], up_w[:, cut], preferred_element_type=F32)

    def pair_copy(unit, half):
        return remote(
            partial.at[unit % 2, 1 - core, :, :, :, part(half)],
            pair_in.at[unit, :, :, :, part(half)],
            pair_send.at[unit, half],
            pair_recv.at[unit, half],
            other,
        )

    def result_copies(unit, half):
        crossing = remote(
            results.at[unit, 1, pl.ds(0, 5), :, part(half)],
            cross_in.at[unit, :, :, part(half)],
            back_ssem.at[unit, half, 0],
            back_rsem.at[unit, half, 0],
            device(1, 0),
        )
        return [crossing] + [
            remote(
                results.at[unit, to, slot, :, part(half)],
                far_in.at[unit, i, :, part(half)],
                back_ssem.at[unit, half, 1 + i],
                back_rsem.at[unit, half, 1 + i],
                device(across, -step),
            )
            for i, (to, slot, across, step) in enumerate(FAR_ROWS)
        ]

    def sum_copies(unit, half, hop):
        return [
            remote(
                sums_out.at[unit % 2, hop, i, :, part(half)],
                sums_in.at[unit, hop, i, :, part(half)],
                back_ssem.at[unit, half, 7 + 2 * hop + i],
                back_rsem.at[unit, half, 7 + 2 * hop + i],
                device(0, step),
            )
            for i, step in enumerate((-1, 1))
        ]

    def combine(unit, half, slot, terms, added, put):
        gated = unit % 2 == 0
        weights = jnp.transpose(
            jnp.concatenate([table[unit, slot, e] for e, _ in terms], axis=0)
        )
        if gated:
            high = weights.astype(BF16)
            low = (weights - high.astype(F32)).astype(BF16)
            matrix = jnp.concatenate([high, low], axis=0)
        else:
            matrix = jnp.where(weights > 0.0, 1.0, 0.0).astype(BF16)

        @over_part(half)
        def _(i):
            cut = columns(i)
            rows = jnp.concatenate([term[:, cut].astype(F32) for _, term in terms], axis=0)
            total = jnp.dot(matrix, rows.astype(BF16), preferred_element_type=F32)
            if gated:
                total = total[:token_rows] + total[token_rows:]
            for extra in added:
                total = total + extra[:, cut].astype(F32)
            put(cut, total)

    def close_terms(unit, slot):
        return [
            (expert(0, 0), results.at[unit, 0, slot]),
            (expert(1, 0), cross_in.at[unit, slot]),
        ]

    def sum_far(unit, half):
        onward = sum_copies(unit, half, 0)
        for copy in result_copies(unit, half):
            copy.wait_recv()
        for i, (slot, steps) in enumerate(FAR_STEPS):
            terms = close_terms(unit, slot) + [
                (expert(*at), far_in.at[unit, 3 * i + n]) for n, at in enumerate(steps)
            ]
            target = sums_out.at[unit % 2, 0, i]

            def put(cut, total):
                target[:, cut] = total.astype(BF16)

            combine(unit, half, slot, terms, [], put)
            onward[i].start()

    def sum_near(unit, half):
        arrivals, onward = sum_copies(unit, half, 0), sum_copies(unit, half, 1)
        for i, slot in enumerate((1, 3)):
            arrivals[i].wait_recv()
            target = sums_out.at[unit % 2, 1, i]

            def put(cut, total):
                target[:, cut] = total.astype(BF16)

            terms = close_terms(unit, slot)
            combine(unit, half, slot, terms, [sums_in.at[unit, 0, i]], put)
            onward[i].start()

    def sum_own(unit):
        def put(cut, total):
            stage[:, cut] = total

        added = [sums_in.at[unit, 1, i] for i in range(2)]
        for half in range(PARTS):
            for copy in sum_copies(unit, half, 1):
                copy.wait_recv()
            combine(unit, half, 2, close_terms(unit, 2), added, put)

    def sums_sent(unit):
        for half in range(PARTS):
            for hop in range(2):
                for copy in sum_copies(unit, half, hop):
                    copy.wait_send()

    def send_back(unit, half):
        pair_copy(unit, half).wait()

        @over_part(half)
        def _(i):
            cut = columns(i)
            mine = partial[unit % 2, core, :, :, :, cut].astype(F32)
            both = mine + pair_in[unit, :, :, :, cut].astype(F32)
            results[unit, :, :, :, cut] = both.astype(BF16)

        for copy in result_copies(unit, half):
            copy.start()

    def outputs(unit, rows):
        for half in range(PARTS):

            @over_part(half)
            def _(i):
                values = rows(columns(i)).reshape(2, 2, ring, slots, wide)
                partial[unit % 2, :, :, :, :, columns(i)] = values.astype(BF16)

            pair_copy(unit, half).start()

    def forward(unit):
        gather(FWD_UNITS[unit // 2])
        project(fwd_gate, fwd_up)
        gate = fwd_gate[...]
        hid_a[...] = (gate * jax.nn.sigmoid(gate) * fwd_up[...]).astype(BF16)
        outputs(
            unit, lambda cut: jnp.dot(hid_a[...], down_w[:, cut], preferred_element_type=F32)
        )

    def recompute(unit):
        gather(ROW_UNITS[unit // 2])
        project(gate_pre, up_pre)

    def backward(unit):
        gather(GRAD_UNITS[unit // 2])
        across = (((1,), (1,)), ((), ()))

        @pl.loop(0, hidden // 256)
        def _(i):
            cut = pl.ds(pl.multiple_of(i * 256, 256), 256)
            grad = lax.dot_general(rows_in[...], down_w[cut, :], across, preferred_element_type=F32)
            gate = gate_pre[:, cut]
            sigmoid = jax.nn.sigmoid(gate)
            hid_a[:, cut] = (
                grad * up_pre[:, cut] * sigmoid * (1.0 + gate * (1.0 - sigmoid))
            ).astype(BF16)
            hid_b[:, cut] = (grad * (gate * sigmoid)).astype(BF16)

        def rows(cut):
            total = lax.dot_general(
                hid_a[...], gate_w[cut, :], across, preferred_element_type=F32
            )
            return total + lax.dot_general(
                hid_b[...], up_w[cut, :], across, preferred_element_type=F32
            )

        outputs(unit, rows)

    def mixture(unit, base, target):
        sum_own(unit)
        target[...] = (base[...].astype(F32) + stage[...]).astype(BF16)

    def input_grad(unit, saved, cotangent, target):
        sum_own(unit)
        weighted = stage[...] * gain[...]
        widened = saved.astype(F32)
        inverse = inverse_rms(widened)
        correction = jnp.mean(weighted * widened, axis=-1, keepdims=True)
        target[...] = (
            cotangent[...].astype(F32)
            + inverse * weighted
            - widened * (inverse * inverse * inverse) * correction
        ).astype(BF16)

    def move(which, source, peer):
        return pltpu.make_async_remote_copy(
            src_ref=source,
            dst_ref=moved.at[which],
            send_sem=pipe_send.at[which],
            recv_sem=pipe_recv.at[which],
            device_id={"pipe": peer},
            device_id_type=MESH,
        )

    need("fwd_ids", "fwd_gates", "bwd_ids", "bwd_gates")
    for batch in range(4):
        begin = 2 * topk * batch
        meta[2, begin : begin + topk, :token_rows] = ids[batch % 2, batch // 2].astype(F32)
        meta[2, begin + topk : begin + 2 * topk, :token_rows] = gates[batch % 2, batch // 2]
    current, cotangent = moved.at[0], moved.at[1]
    forth = move(0, outs.at[0], after)
    upward = move(1, grads, before)

    def begin_spread(unit):
        if unit == 0:
            need("fwd_state", "gain")
            held[0, 2] = normalize(inputs[0])
        elif unit == 1:
            need("saved0", "gain")
            held[1, 2] = normalize(inputs[2])
        elif unit == 2:
            need("grad_state")
        elif unit == 3:
            need("saved1", "gain")
            held[3, 2] = normalize(inputs[3])
        elif unit == 4:
            need("new_tokens")
            forth.wait()
            current[...] = jnp.where(pipe == 0, inputs[1], current[...])
            held[4, 2] = normalize(current[...])
            release(0)
            sums_sent(0)
        else:
            need("new_grads")
            upward.wait()
            cotangent[...] = jnp.where(pipe == sections - 1, inputs[4], cotangent[...])
            held[5, 2] = cotangent[...]
            release(2)
            sums_sent(1)
        spread(unit)

    def tables(_):
        for copy in meta_copies:
            copy.wait_recv()

        @pl.loop(0, 5)
        def _(slot):
            for batch in range(4):
                begin = 2 * topk * batch
                weights = slot_weights(
                    meta[slot, begin : begin + topk, :token_rows],
                    meta[slot, begin + topk : begin + 2 * topk, :token_rows],
                )
                table[batch, slot] = weights.reshape(chips, slots, token_rows)

        need("gate", "up", "down")

    finals = [
        pltpu.make_async_copy(outs.at[i], target.at[0], output_sem.at[i])
        for i, target in enumerate((fwd_out, grad_out))
    ]

    def complete(unit):
        if unit == 0:
            mixture(0, inputs.at[0], outs.at[0])
            forth.start()
        elif unit == 1:
            input_grad(1, inputs[2], held.at[2, 2], grads)
            upward.start()
        elif unit == 2:
            mixture(2, current, outs.at[0])
            finals[0].start()
        else:
            input_grad(3, inputs[3], cotangent, outs.at[1])
            finals[1].start()

    pl.semaphore_wait(barrier, chips + 2)
    for copy in meta_copies:
        copy.start()
    steps = {
        "spread": begin_spread,
        "tables": tables,
        "relay": relay,
        "finish": finish,
        "collect": collect,
        "forward": forward,
        "recompute": recompute,
        "backward": backward,
        "back": send_back,
        "far": sum_far,
        "near": sum_near,
        "own": complete,
    }
    for name, *which in ORDER:
        steps[name](*which)
    for copy in finals:
        copy.wait()

    for copy in meta_copies:
        copy.wait_send()
    for unit in range(6):
        for half in range(PARTS):
            for copy in first_hop(unit, half) + second_hop(unit, half):
                copy.wait_send()
    for unit in (4, 1, 5, 3):
        release(unit)
    for unit in (2, 3):
        sums_sent(unit)
    for unit in range(4):
        for half in range(PARTS):
            for copy in result_copies(unit, half):
                copy.wait_send()


def hand_over(first, second, first_out, second_out, held, in_sems, out_sems):
    pairs = enumerate(((first, first_out), (second, second_out)))
    arrive, leave = [], []
    for i, (source, target) in pairs:
        for half in range(PARTS):
            size = held.shape[-1] // PARTS
            cut = pl.ds(half * size, size)
            between = held.at[i, :, :, cut]
            arrive.append(
                pltpu.make_async_copy(source.at[:, :, cut], between, in_sems.at[i, half])
            )
            leave.append(
                pltpu.make_async_copy(between, target.at[:, :, cut], out_sems.at[i, half])
            )
    for copy in arrive:
        copy.start()
    for before, after in zip(arrive, leave):
        before.wait()
        after.start()
    for copy in leave:
        copy.wait()


def shards(*arrays):
    fwd_state, fwd_ids, w_gate = arrays[0], arrays[9], arrays[6]
    token_rows, width = fwd_state.shape[1:]
    hidden = w_gate.shape[2]
    chips = lax.axis_size("expert") // 2
    topk = fwd_ids.shape[3]
    slots = token_rows * topk // chips
    count = 2 * chips * slots
    dma = pltpu.SemaphoreType.DMA
    hbm = pl.BlockSpec(memory_space=pl.ANY)
    row = jax.ShapeDtypeStruct(fwd_state.shape, BF16)
    routes = [jnp.transpose(array, (0, 1, 3, 2)) for array in arrays[9:]]
    results = pl.pallas_call(
        kernel,
        out_shape=(row, row),
        in_specs=[hbm] * len(arrays),
        out_specs=(hbm, hbm),
        scratch_shapes=[
            pltpu.VMEM((5, token_rows, width), BF16),
            pltpu.VMEM((1, width), F32),
            pltpu.VMEM((2, 2, topk, token_rows), jnp.int32),
            pltpu.VMEM((2, 2, topk, token_rows), F32),
            pltpu.VMEM((2, token_rows, width), BF16),
            dma((14,)),
            dma((2,)),
            pltpu.VMEM((width, hidden), BF16),
            pltpu.VMEM((width, hidden), BF16),
            pltpu.VMEM((hidden, width), BF16),
            pltpu.VMEM((5, 8 * topk, 128), F32),
            pltpu.VMEM((4, 5, chips, slots, token_rows), F32),
            pltpu.VMEM((6, 5, token_rows, width), BF16),
            pltpu.VMEM((4, 5, slots, width), BF16),
            pltpu.VMEM((4, 6, slots, width), BF16),
            pltpu.VMEM((6, 2, 2, chips // 2, slots, width), BF16),
            pltpu.VMEM((2, 2, 2, chips // 2, slots, width), BF16),
            pltpu.VMEM((4, 2, chips // 2, slots, width), BF16),
            pltpu.VMEM((4, 2, chips // 2, slots, width), BF16),
            pltpu.VMEM((4, 5, slots, width), BF16),
            pltpu.VMEM((4, 6, slots, width), BF16),
            pltpu.VMEM((4, 2, 2, token_rows, width), BF16),
            pltpu.VMEM((2, 2, 2, token_rows, width), BF16),
            pltpu.VMEM((count, width), BF16),
            pltpu.VMEM((count, hidden), F32),
            pltpu.VMEM((count, hidden), F32),
            pltpu.VMEM((count, hidden), F32),
            pltpu.VMEM((count, hidden), F32),
            pltpu.VMEM((count, hidden), BF16),
            pltpu.VMEM((count, hidden), BF16),
            pltpu.VMEM((token_rows, width), F32),
            pltpu.VMEM((2, token_rows, width), BF16),
            pltpu.VMEM((token_rows, width), BF16),
            dma((4,)),
            dma((4,)),
            dma((6, PARTS, 13)),
            dma((6, PARTS, 13)),
            dma((6, PARTS)),
            dma((6, PARTS)),
            dma((4, PARTS)),
            dma((4, PARTS)),
            dma((4, PARTS, 11)),
            dma((4, PARTS, 11)),
            dma((2,)),
            dma((2,)),
        ],
        compiler_params=pltpu.CompilerParams(
            collective_id=0, has_side_effects=True, vmem_limit_bytes=60 * 2**20
        ),
        name="relay",
    )(*arrays[:9], *routes)
    return pl.pallas_call(
        hand_over,
        out_shape=(row, row),
        in_specs=[hbm] * 2,
        out_specs=(hbm, hbm),
        scratch_shapes=[
            pltpu.VMEM((2, *fwd_state.shape), BF16),
            dma((2, PARTS)),
            dma((2, PARTS)),
        ],
        name="hand_over",
    )(*results)


def solution(mesh):
    placed = (
        P("pipe", "expert", None),
        P(None, "expert", None),
        P(None, "pipe", "expert", None),
        P("pipe", "expert", None),
        P(None, "expert", None),
        P("pipe", None),
        P("pipe", None, "expert"),
        P("pipe", None, "expert"),
        P("pipe", "expert", None),
        P(None, "pipe", "expert", None),
        P(None, "pipe", "expert", None),
        P(None, "pipe", "expert", None),
        P(None, "pipe", "expert", None),
    )
    return jax.shard_map(
        shards,
        mesh=mesh,
        in_specs=placed,
        out_specs=(P("pipe", "expert", None), P("pipe", "expert", None)),
        check_vma=False,
    )
```

```python
import functools

import jax
import jax.numpy as jnp
from jax import lax
from jax.experimental import pallas as pl
from jax.experimental.pallas import tpu as pltpu
from jax.sharding import PartitionSpec as P

MESH = pl.DeviceIdType.MESH
F32 = jnp.float32
BF16 = jnp.bfloat16
PARTS = 2
BATCHES = (0, 1, 1, 3, 2, 3)
SCALED = (False, False, True, False, False, True)
LOTS = (0, 1, 2, 3, 0, 2)
FWD_UNITS, ROW_UNITS, GRAD_UNITS = (0, 4), (1, 3), (2, 5)
FAR_ROWS = (
    (0, 7, 0, 1),
    (1, 7, 1, 1),
    (0, 6, 0, 2),
    (0, 5, 0, -1),
    (1, 5, 1, -1),
    (1, 6, 1, -2),
)
FAR_STEPS = ((0, ((0, 1), (1, 1), (0, 2))), (4, ((0, -1), (1, -1), (1, -2))))

ORDER = (
    ("spread", 2),
    ("spread", 0),
    ("tables", 0),
    ("spread", 1),
    ("relay", 0, 1),
    ("relay", 0, 0),
    ("relay", 1, 0),
    ("finish", 0, 1),
    ("finish", 0, 0),
    ("relay", 1, 1),
    ("relay", 2, 1),
    ("relay", 2, 0),
    ("finish", 1, 0),
    ("collect", 0, 0),
    ("collect", 0, 1),
    ("finish", 1, 1),
    ("forward", 0),
    ("finish", 2, 0),
    ("collect", 1, 0),
    ("finish", 2, 1),
    ("back", 0, 0),
    ("collect", 2, 0),
    ("collect", 1, 1),
    ("back", 0, 1),
    ("spread", 3),
    ("collect", 2, 1),
    ("recompute", 1),
    ("far", 0, 0),
    ("backward", 1),
    ("far", 0, 1),
    ("back", 1, 1),
    ("near", 0, 0),
    ("back", 1, 0),
    ("near", 0, 1),
    ("far", 1, 1),
    ("far", 1, 0),
    ("own", 0),
    ("relay", 3, 0),
    ("near", 1, 1),
    ("near", 1, 0),
    ("relay", 3, 1),
    ("spread", 4),
    ("own", 1),
    ("finish", 3, 0),
    ("relay", 4, 0),
    ("relay", 4, 1),
    ("spread", 5),
    ("finish", 4, 1),
    ("finish", 4, 0),
    ("relay", 5, 1),
    ("collect", 4, 1),
    ("collect", 3, 0),
    ("relay", 5, 0),
    ("finish", 3, 1),
    ("collect", 4, 0),
    ("finish", 5, 1),
    ("forward", 2),
    ("finish", 5, 0),
    ("back", 2, 0),
    ("collect", 3, 1),
    ("collect", 5, 1),
    ("recompute", 3),
    ("back", 2, 1),
    ("collect", 5, 0),
    ("settle", 0),
    ("far", 2, 0),
    ("backward", 3),
    ("far", 2, 1),
    ("back", 3, 0),
    ("back", 3, 1),
    ("settle", 1),
    ("near", 2, 1),
    ("far", 3, 0),
    ("far", 3, 1),
    ("near", 2, 0),
    ("near", 3, 0),
    ("near", 3, 1),
    ("own", 2),
    ("own", 3),
)


def kernel(
    fwd_state,
    new_tokens,
    saved_input,
    grad_state,
    new_grads,
    norm_gain,
    w_gate,
    w_up,
    w_down,
    fwd_ids,
    fwd_gates,
    bwd_ids,
    bwd_gates,
    fwd_out,
    grad_out,
    inputs,
    gain,
    ids,
    gates,
    outs,
    input_sem,
    output_sem,
    gate_w,
    up_w,
    down_w,
    meta,
    table,
    held,
    cross,
    far,
    recv,
    partial,
    pair_in,
    results,
    cross_in,
    far_in,
    sums_in,
    sums_out,
    rows_in,
    fwd_gate,
    fwd_up,
    gate_pre,
    up_pre,
    hid_a,
    hid_b,
    stage,
    moved,
    grads,
    meta_send,
    meta_recv,
    row_send,
    row_recv,
    swap_send,
    swap_recv,
    pair_send,
    pair_recv,
    back_ssem,
    back_rsem,
    pipe_send,
    pipe_recv,
):
    pipe = lax.axis_index("pipe")
    sections = lax.axis_size("pipe")
    me = lax.axis_index("expert")
    chips = lax.axis_size("expert") // 2
    chip = me // 2
    core = me % 2
    ring = chips // 2
    column = chip // ring
    plane = chip % ring
    other = chip * 2 + 1 - core
    width = fwd_state.shape[-1]
    token_rows = fwd_state.shape[-2]
    topk = fwd_ids.shape[-2]
    slots = recv.shape[4]
    count = chips * slots
    hidden = gate_w.shape[1]
    wide = 256 if width // PARTS % 256 == 0 else width // PARTS
    after = lax.rem(pipe + 1, sections)
    before = lax.rem(pipe + sections - 1, sections)

    barrier = pltpu.get_barrier_semaphore()

    @pl.loop(1, chips)
    def _(j):
        peer = lax.rem(chip + j, chips) * 2 + core
        pl.semaphore_signal(barrier, inc=1, device_id={"expert": peer}, device_id_type=MESH)

    pl.semaphore_signal(barrier, inc=1, device_id={"expert": other}, device_id_type=MESH)
    pl.semaphore_signal(barrier, inc=1, device_id={"pipe": after}, device_id_type=MESH)
    pl.semaphore_signal(barrier, inc=1, device_id={"pipe": before}, device_id_type=MESH)

    sources = {
        "fwd_ids": (fwd_ids.at[:, 0], ids.at[0]),
        "fwd_gates": (fwd_gates.at[:, 0], gates.at[0]),
        "bwd_ids": (bwd_ids.at[:, 0], ids.at[1]),
        "bwd_gates": (bwd_gates.at[:, 0], gates.at[1]),
        "grad_state": (grad_state.at[0], held.at[2, 2]),
        "gain": (norm_gain, gain),
        "saved0": (saved_input.at[0, 0], inputs.at[2]),
        "fwd_state": (fwd_state.at[0], inputs.at[0]),
        "saved1": (saved_input.at[1, 0], inputs.at[3]),
        "gate": (w_gate.at[0], gate_w),
        "up": (w_up.at[0], up_w),
        "down": (w_down.at[0], down_w),
        "new_tokens": (new_tokens.at[0], inputs.at[1]),
        "new_grads": (new_grads.at[0], inputs.at[4]),
    }
    loads = {
        key: pltpu.make_async_copy(source, target, input_sem.at[i])
        for i, (key, (source, target)) in enumerate(sources.items())
    }
    for load in loads.values():
        load.start()

    def need(*keys):
        for key in keys:
            if key in loads:
                loads.pop(key).wait()

    def columns(i):
        return pl.ds(pl.multiple_of(i * wide, wide), wide)

    def part(half):
        return pl.ds(half * (width // PARTS), width // PARTS)

    def over_part(half):
        steps = width // PARTS // wide
        return pl.loop(half * steps, (half + 1) * steps, unroll=True)

    def device(across, step):
        to_column = lax.rem(column + across, 2)
        to_plane = lax.rem(plane + step + 2 * ring, ring)
        return (to_column * ring + to_plane) * 2 + core

    def expert(across, step):
        return device(across, step) // 2

    def remote(source, target, sends, receives, peer):
        return pltpu.make_async_remote_copy(
            src_ref=source,
            dst_ref=target,
            send_sem=sends,
            recv_sem=receives,
            device_id={"expert": peer},
            device_id_type=MESH,
        )

    def slot_weights(ids, gates):
        named = lax.broadcasted_iota(jnp.int32, (count, token_rows), 0) // slots
        place = lax.broadcasted_iota(jnp.int32, (count, token_rows), 0) % slots
        named = named.astype(F32)
        chosen = jnp.zeros((count, token_rows), F32)
        weight = jnp.zeros((count, token_rows), F32)
        for k in range(topk):
            hit = ids[k : k + 1] == named
            chosen = jnp.where(hit, 1.0, chosen)
            weight = jnp.where(hit, gates[k : k + 1], weight)
        row = lax.broadcasted_iota(jnp.int32, (token_rows, token_rows), 0)
        col = lax.broadcasted_iota(jnp.int32, (token_rows, token_rows), 1)
        earlier = jnp.where(row < col, 1.0, 0.0).astype(BF16)
        rank = jnp.dot(chosen.astype(BF16), earlier, preferred_element_type=F32)
        return jnp.where(rank == place.astype(F32), weight, 0.0)

    def inverse_rms(widened):
        return lax.rsqrt(jnp.mean(widened * widened, axis=-1, keepdims=True) + 1e-06)

    def normalize(values):
        widened = values.astype(F32)
        return (widened * inverse_rms(widened) * gain[...]).astype(BF16)

    meta_copies = [
        remote(meta.at[2], meta.at[2 - step], meta_send.at[i], meta_recv.at[i], device(0, step))
        for i, step in enumerate((1, -1, 2, -2))
    ]

    def first_hop(unit, half):
        return [
            remote(
                held.at[unit, 2, :, part(half)],
                held.at[unit, 2 - step, :, part(half)],
                row_send.at[unit, half, i],
                row_recv.at[unit, half, i],
                device(0, step),
            )
            for i, step in enumerate((1, -1))
        ]

    def second_hop(unit, half):
        return [
            remote(
                held.at[unit, 2 - step, :, part(half)],
                held.at[unit, 2 - 2 * step, :, part(half)],
                row_send.at[unit, half, 2 + i],
                row_recv.at[unit, half, 2 + i],
                device(0, step),
            )
            for i, step in enumerate((1, -1))
        ]

    def cross_copies(unit, half):
        return [
            remote(
                cross.at[LOTS[unit], slots_of, :, part(half)],
                recv.at[unit, core, 1, slots_of, :, part(half)],
                row_send.at[unit, half, 4 + i],
                row_recv.at[unit, half, 4 + i],
                device(1, 0),
            )
            for i, slots_of in enumerate((pl.ds(1, 3), pl.ds(0, 1), pl.ds(4, 1)))
        ]

    def far_copies(unit, half):
        return [
            remote(
                far.at[LOTS[unit], i, :, part(half)],
                recv.at[unit, core, to, slot, :, part(half)],
                row_send.at[unit, half, 7 + i],
                row_recv.at[unit, half, 7 + i],
                device(across, step),
            )
            for i, (to, slot, across, step) in enumerate(FAR_ROWS)
        ]

    def pick(unit, half, first, many, targets):
        share = len(targets) // many
        batch, scaled = BATCHES[unit], SCALED[unit]
        picked = jnp.concatenate(
            [table[batch, first + n // share, e] for n, (e, _) in enumerate(targets)], axis=0
        )
        scale = jnp.sum(picked, axis=1, keepdims=True)
        if many > 1:
            picked = jnp.concatenate([picked] * many, axis=1)
            row = lax.broadcasted_iota(jnp.int32, picked.shape, 0) // (share * slots)
            col = lax.broadcasted_iota(jnp.int32, picked.shape, 1) // token_rows
            picked = jnp.where(row == col, picked, 0.0)
        select = jnp.where(picked > 0.0, 1.0, 0.0).astype(BF16)

        @over_part(half)
        def _(i):
            cut = columns(i)
            block = held[unit, pl.ds(first, many), :, cut].reshape(many * token_rows, wide)
            rows = jnp.dot(select, block, preferred_element_type=F32)
            if scaled:
                rows = rows * scale
            for n, (_, target) in enumerate(targets):
                target[:, cut] = rows[n * slots : (n + 1) * slots].astype(BF16)

    def near(unit, slot):
        return [
            (expert(0, 0), recv.at[unit, core, 0, slot]),
            (expert(1, 0), cross.at[LOTS[unit], slot]),
        ]

    def spread(unit):
        for half in range(PARTS):
            for copy in first_hop(unit, half):
                copy.start()

    def relay(unit, half):
        arrivals, onward = first_hop(unit, half), second_hop(unit, half)
        for i in range(2):
            arrivals[i].wait_recv()
            onward[i].start()
        targets = [target for slot in (1, 2, 3) for target in near(unit, slot)]
        pick(unit, half, 1, 3, targets)
        cross_copies(unit, half)[0].start()

    def finish(unit, half):
        arrivals, beyond = second_hop(unit, half), far_copies(unit, half)
        crossing = cross_copies(unit, half)
        for i, (slot, steps) in enumerate(FAR_STEPS):
            arrivals[i].wait_recv()
            targets = [
                (expert(*at), far.at[LOTS[unit], 3 * i + n]) for n, at in enumerate(steps)
            ]
            pick(unit, half, slot, 1, targets)
            for n in range(3):
                beyond[3 * i + n].start()
        for i, slot in enumerate((0, 4)):
            pick(unit, half, slot, 1, near(unit, slot))
            crossing[1 + i].start()

    def release(unit):
        for half in range(PARTS):
            for copy in cross_copies(unit, half) + far_copies(unit, half):
                copy.wait_send()

    def swap_copy(unit, half, rail):
        half_rows = recv.at[unit, rail, :, :, :, part(half)]
        return remote(
            half_rows, half_rows, swap_send.at[unit, half], swap_recv.at[unit, half], other
        )

    def collect(unit, half):
        for copy in cross_copies(unit, half) + far_copies(unit, half):
            copy.wait_recv()
        swap_copy(unit, half, core).start()

    def gather(unit):
        for half in range(PARTS):
            swap_copy(unit, half, 1 - core).wait_recv()
            swap_copy(unit, half, core).wait_send()

            @over_part(half)
            def _(i):
                cut = columns(i)
                block = recv[unit, :, :, :, :, cut].astype(F32)
                rows_in[:, cut] = block.reshape(2 * count, wide).astype(BF16)

    def project(gate_to, up_to):
        @pl.loop(0, hidden // 256)
        def _(i):
            cut = pl.ds(pl.multiple_of(i * 256, 256), 256)
            gate_to[:, cut] = jnp.dot(rows_in[...], gate_w[:, cut], preferred_element_type=F32)
            up_to[:, cut] = jnp.dot(rows_in[...], up_w[:, cut], preferred_element_type=F32)

    def pair_copy(unit, half):
        return remote(
            partial.at[unit % 2, 1 - core, :, :, :, part(half)],
            pair_in.at[unit, :, :, :, part(half)],
            pair_send.at[unit, half],
            pair_recv.at[unit, half],
            other,
        )

    def result_copies(unit, half):
        straight = [
            remote(
                results.at[unit, to, slot, :, part(half)],
                far_in.at[unit, i, :, part(half)],
                back_ssem.at[unit, half, i],
                back_rsem.at[unit, half, i],
                device(across, -step),
            )
            for i, (to, slot, across, step) in enumerate(FAR_ROWS)
        ]
        crossing = [
            remote(
                results.at[unit, 1, slots_of, :, part(half)],
                cross_in.at[unit, slots_of, :, part(half)],
                back_ssem.at[unit, half, 6 + i],
                back_rsem.at[unit, half, 6 + i],
                device(1, 0),
            )
            for i, slots_of in enumerate((pl.ds(0, 1), pl.ds(4, 1), pl.ds(1, 3)))
        ]
        return straight + crossing

    def sum_copies(unit, half, hop):
        return [
            remote(
                sums_out.at[unit % 2, hop, i, :, part(half)],
                sums_in.at[unit, hop, i, :, part(half)],
                back_ssem.at[unit, half, 9 + 2 * hop + i],
                back_rsem.at[unit, half, 9 + 2 * hop + i],
                device(0, step),
            )
            for i, step in enumerate((-1, 1))
        ]

    def combine(unit, half, slot, terms, added, put):
        gated = unit % 2 == 0
        weights = jnp.transpose(
            jnp.concatenate([table[unit, slot, e] for e, _ in terms], axis=0)
        )
        if gated:
            high = weights.astype(BF16)
            low = (weights - high.astype(F32)).astype(BF16)
            matrix = jnp.concatenate([high, low], axis=0)
        else:
            matrix = jnp.where(weights > 0.0, 1.0, 0.0).astype(BF16)

        @over_part(half)
        def _(i):
            cut = columns(i)
            rows = jnp.concatenate([term[:, cut].astype(F32) for _, term in terms], axis=0)
            total = jnp.dot(matrix, rows.astype(BF16), preferred_element_type=F32)
            if gated:
                total = total[:token_rows] + total[token_rows:]
            for extra in added:
                total = total + extra[:, cut].astype(F32)
            put(cut, total)

    def close_terms(unit, slot):
        return [
            (expert(0, 0), results.at[unit, 0, slot]),
            (expert(1, 0), cross_in.at[unit, slot]),
        ]

    def sum_far(unit, half):
        onward = sum_copies(unit, half, 0)
        for copy in result_copies(unit, half)[:8]:
            copy.wait_recv()
        for i, (slot, steps) in enumerate(FAR_STEPS):
            terms = close_terms(unit, slot) + [
                (expert(*at), far_in.at[unit, 3 * i + n]) for n, at in enumerate(steps)
            ]
            target = sums_out.at[unit % 2, 0, i]

            def put(cut, total):
                target[:, cut] = total.astype(BF16)

            combine(unit, half, slot, terms, [], put)
            onward[i].start()

    def sum_near(unit, half):
        arrivals, onward = sum_copies(unit, half, 0), sum_copies(unit, half, 1)
        result_copies(unit, half)[8].wait_recv()
        for i, slot in enumerate((1, 3)):
            arrivals[i].wait_recv()
            target = sums_out.at[unit % 2, 1, i]

            def put(cut, total):
                target[:, cut] = total.astype(BF16)

            terms = close_terms(unit, slot)
            combine(unit, half, slot, terms, [sums_in.at[unit, 0, i]], put)
            onward[i].start()

    def sum_own(unit):
        def put(cut, total):
            stage[:, cut] = total

        added = [sums_in.at[unit, 1, i] for i in range(2)]
        for half in range(PARTS):
            for copy in sum_copies(unit, half, 1):
                copy.wait_recv()
            combine(unit, half, 2, close_terms(unit, 2), added, put)

    def sums_sent(unit):
        for half in range(PARTS):
            for hop in range(2):
                for copy in sum_copies(unit, half, hop):
                    copy.wait_send()

    def send_back(unit, half):
        pair_copy(unit, half).wait()

        @over_part(half)
        def _(i):
            cut = columns(i)
            mine = partial[unit % 2, core, :, :, :, cut].astype(F32)
            both = mine + pair_in[unit, :, :, :, cut].astype(F32)
            results[unit, :, :, :, cut] = both.astype(BF16)

        for copy in result_copies(unit, half):
            copy.start()

    def outputs(unit, rows):
        for half in range(PARTS):

            @over_part(half)
            def _(i):
                values = rows(columns(i)).reshape(2, 2, ring, slots, wide)
                partial[unit % 2, :, :, :, :, columns(i)] = values.astype(BF16)

            pair_copy(unit, half).start()

    def forward(unit):
        gather(FWD_UNITS[unit // 2])
        project(fwd_gate, fwd_up)
        gate = fwd_gate[...]
        hid_a[...] = (gate * jax.nn.sigmoid(gate) * fwd_up[...]).astype(BF16)
        outputs(
            unit, lambda cut: jnp.dot(hid_a[...], down_w[:, cut], preferred_element_type=F32)
        )

    def recompute(unit):
        gather(ROW_UNITS[unit // 2])
        project(gate_pre, up_pre)

    def backward(unit):
        gather(GRAD_UNITS[unit // 2])
        across = (((1,), (1,)), ((), ()))

        @pl.loop(0, hidden // 256)
        def _(i):
            cut = pl.ds(pl.multiple_of(i * 256, 256), 256)
            grad = lax.dot_general(rows_in[...], down_w[cut, :], across, preferred_element_type=F32)
            gate = gate_pre[:, cut]
            sigmoid = jax.nn.sigmoid(gate)
            hid_a[:, cut] = (
                grad * up_pre[:, cut] * sigmoid * (1.0 + gate * (1.0 - sigmoid))
            ).astype(BF16)
            hid_b[:, cut] = (grad * (gate * sigmoid)).astype(BF16)

        def rows(cut):
            total = lax.dot_general(
                hid_a[...], gate_w[cut, :], across, preferred_element_type=F32
            )
            return total + lax.dot_general(
                hid_b[...], up_w[cut, :], across, preferred_element_type=F32
            )

        outputs(unit, rows)

    def mixture(unit, base, target):
        sum_own(unit)
        target[...] = (base[...].astype(F32) + stage[...]).astype(BF16)

    def input_grad(unit, saved, cotangent, target):
        inverse = inverse_rms(saved.astype(F32))
        sum_own(unit)
        weighted = stage[...] * gain[...]
        widened = saved.astype(F32)
        correction = jnp.mean(weighted * widened, axis=-1, keepdims=True)
        target[...] = (
            cotangent[...].astype(F32)
            + inverse * weighted
            - widened * (inverse * inverse * inverse) * correction
        ).astype(BF16)

    def move(which, source, peer):
        return pltpu.make_async_remote_copy(
            src_ref=source,
            dst_ref=moved.at[which],
            send_sem=pipe_send.at[which],
            recv_sem=pipe_recv.at[which],
            device_id={"pipe": peer},
            device_id_type=MESH,
        )

    need("fwd_ids", "fwd_gates", "bwd_ids", "bwd_gates")
    for batch in range(4):
        begin = 2 * topk * batch
        meta[2, begin : begin + topk, :token_rows] = ids[batch % 2, batch // 2].astype(F32)
        meta[2, begin + topk : begin + 2 * topk, :token_rows] = gates[batch % 2, batch // 2]
    current, cotangent = moved.at[0], moved.at[1]
    forth = move(0, outs.at[0], after)
    upward = move(1, grads, before)

    def begin_spread(unit):
        if unit == 0:
            need("fwd_state", "gain")
            held[0, 2] = normalize(inputs[0])
        elif unit == 1:
            need("saved0", "gain")
            held[1, 2] = normalize(inputs[2])
        elif unit == 2:
            need("grad_state")
        elif unit == 3:
            need("saved1", "gain")
            held[3, 2] = normalize(inputs[3])
        elif unit == 4:
            need("new_tokens")
            forth.wait()
            current[...] = jnp.where(pipe == 0, inputs[1], current[...])
            held[4, 2] = normalize(current[...])
            release(0)
            sums_sent(0)
        else:
            need("new_grads")
            upward.wait()
            cotangent[...] = jnp.where(pipe == sections - 1, inputs[4], cotangent[...])
            held[5, 2] = cotangent[...]
            release(2)
            sums_sent(1)
        spread(unit)

    def tables(_):
        for copy in meta_copies:
            copy.wait_recv()

        @pl.loop(0, 5)
        def _(slot):
            for batch in range(4):
                begin = 2 * topk * batch
                weights = slot_weights(
                    meta[slot, begin : begin + topk, :token_rows],
                    meta[slot, begin + topk : begin + 2 * topk, :token_rows],
                )
                table[batch, slot] = weights.reshape(chips, slots, token_rows)

        need("gate", "up", "down")

    finals = [
        pltpu.make_async_copy(outs.at[i], target.at[0], output_sem.at[i])
        for i, target in enumerate((fwd_out, grad_out))
    ]

    def complete(unit):
        if unit == 0:
            mixture(0, inputs.at[0], outs.at[0])
            forth.start()
        elif unit == 1:
            input_grad(1, inputs[2], held.at[2, 2], grads)
            upward.start()
        elif unit == 2:
            mixture(2, current, outs.at[0])
            finals[0].start()
        else:
            input_grad(3, inputs[3], cotangent, outs.at[1])
            finals[1].start()

    pl.semaphore_wait(barrier, chips + 2)
    for copy in meta_copies:
        copy.start()
    def hops_sent(unit):
        for half in range(PARTS):
            for copy in first_hop(unit, half) + second_hop(unit, half):
                copy.wait_send()

    def results_sent(unit):
        for half in range(PARTS):
            for copy in result_copies(unit, half):
                copy.wait_send()

    def settle(stage):
        if stage == 0:
            for copy in meta_copies:
                copy.wait_send()
            for unit in range(4):
                hops_sent(unit)
            for unit in (1, 3):
                release(unit)
            for unit in (0, 1):
                results_sent(unit)
        elif stage == 1:
            for unit in (4, 5):
                hops_sent(unit)
                release(unit)
        else:
            for unit in (2, 3):
                results_sent(unit)
                sums_sent(unit)

    steps = {
        "settle": settle,
        "spread": begin_spread,
        "tables": tables,
        "relay": relay,
        "finish": finish,
        "collect": collect,
        "forward": forward,
        "recompute": recompute,
        "backward": backward,
        "back": send_back,
        "far": sum_far,
        "near": sum_near,
        "own": complete,
    }
    for name, *which in ORDER:
        steps[name](*which)
    settle(2)
    for copy in finals:
        copy.wait()


def hand_over(first, second, first_out, second_out, held, in_sems, out_sems):
    pairs = enumerate(((first, first_out), (second, second_out)))
    arrive, leave = [], []
    for i, (source, target) in pairs:
        for half in range(PARTS):
            size = held.shape[-1] // PARTS
            cut = pl.ds(half * size, size)
            between = held.at[i, :, :, cut]
            arrive.append(
                pltpu.make_async_copy(source.at[:, :, cut], between, in_sems.at[i, half])
            )
            leave.append(
                pltpu.make_async_copy(between, target.at[:, :, cut], out_sems.at[i, half])
            )
    for copy in arrive:
        copy.start()
    for before, after in zip(arrive, leave):
        before.wait()
        after.start()
    for copy in leave:
        copy.wait()


def shards(*arrays):
    fwd_state, fwd_ids, w_gate = arrays[0], arrays[9], arrays[6]
    token_rows, width = fwd_state.shape[1:]
    hidden = w_gate.shape[2]
    chips = lax.axis_size("expert") // 2
    topk = fwd_ids.shape[3]
    slots = token_rows * topk // chips
    count = 2 * chips * slots
    dma = pltpu.SemaphoreType.DMA
    hbm = pl.BlockSpec(memory_space=pl.ANY)
    row = jax.ShapeDtypeStruct(fwd_state.shape, BF16)
    routes = [jnp.transpose(array, (0, 1, 3, 2)) for array in arrays[9:]]
    results = pl.pallas_call(
        kernel,
        out_shape=(row, row),
        in_specs=[hbm] * len(arrays),
        out_specs=(hbm, hbm),
        scratch_shapes=[
            pltpu.VMEM((5, token_rows, width), BF16),
            pltpu.VMEM((1, width), F32),
            pltpu.VMEM((2, 2, topk, token_rows), jnp.int32),
            pltpu.VMEM((2, 2, topk, token_rows), F32),
            pltpu.VMEM((2, token_rows, width), BF16),
            dma((14,)),
            dma((2,)),
            pltpu.VMEM((width, hidden), BF16),
            pltpu.VMEM((width, hidden), BF16),
            pltpu.VMEM((hidden, width), BF16),
            pltpu.VMEM((5, 8 * topk, 128), F32),
            pltpu.VMEM((4, 5, chips, slots, token_rows), F32),
            pltpu.VMEM((6, 5, token_rows, width), BF16),
            pltpu.VMEM((4, 5, slots, width), BF16),
            pltpu.VMEM((4, 6, slots, width), BF16),
            pltpu.VMEM((6, 2, 2, chips // 2, slots, width), BF16),
            pltpu.VMEM((2, 2, 2, chips // 2, slots, width), BF16),
            pltpu.VMEM((4, 2, chips // 2, slots, width), BF16),
            pltpu.VMEM((4, 2, chips // 2, slots, width), BF16),
            pltpu.VMEM((4, 5, slots, width), BF16),
            pltpu.VMEM((4, 6, slots, width), BF16),
            pltpu.VMEM((4, 2, 2, token_rows, width), BF16),
            pltpu.VMEM((2, 2, 2, token_rows, width), BF16),
            pltpu.VMEM((count, width), BF16),
            pltpu.VMEM((count, hidden), F32),
            pltpu.VMEM((count, hidden), F32),
            pltpu.VMEM((count, hidden), F32),
            pltpu.VMEM((count, hidden), F32),
            pltpu.VMEM((count, hidden), BF16),
            pltpu.VMEM((count, hidden), BF16),
            pltpu.VMEM((token_rows, width), F32),
            pltpu.VMEM((2, token_rows, width), BF16),
            pltpu.VMEM((token_rows, width), BF16),
            dma((4,)),
            dma((4,)),
            dma((6, PARTS, 13)),
            dma((6, PARTS, 13)),
            dma((6, PARTS)),
            dma((6, PARTS)),
            dma((4, PARTS)),
            dma((4, PARTS)),
            dma((4, PARTS, 13)),
            dma((4, PARTS, 13)),
            dma((2,)),
            dma((2,)),
        ],
        compiler_params=pltpu.CompilerParams(
            collective_id=0, has_side_effects=True, vmem_limit_bytes=60 * 2**20
        ),
        name="relay",
    )(*arrays[:9], *routes)
    return pl.pallas_call(
        hand_over,
        out_shape=(row, row),
        in_specs=[hbm] * 2,
        out_specs=(hbm, hbm),
        scratch_shapes=[
            pltpu.VMEM((2, *fwd_state.shape), BF16),
            dma((2, PARTS)),
            dma((2, PARTS)),
        ],
        name="hand_over",
    )(*results)


def solution(mesh):
    placed = (
        P("pipe", "expert", None),
        P(None, "expert", None),
        P(None, "pipe", "expert", None),
        P("pipe", "expert", None),
        P(None, "expert", None),
        P("pipe", None),
        P("pipe", None, "expert"),
        P("pipe", None, "expert"),
        P("pipe", "expert", None),
        P(None, "pipe", "expert", None),
        P(None, "pipe", "expert", None),
        P(None, "pipe", "expert", None),
        P(None, "pipe", "expert", None),
    )
    return jax.shard_map(
        shards,
        mesh=mesh,
        in_specs=placed,
        out_specs=(P("pipe", "expert", None), P("pipe", "expert", None)),
        check_vma=False,
    )
```

```python
import functools

import jax
import jax.numpy as jnp
from jax import lax
from jax.experimental import pallas as pl
from jax.experimental.pallas import tpu as pltpu
from jax.sharding import PartitionSpec as P

MESH = pl.DeviceIdType.MESH
F32 = jnp.float32
BF16 = jnp.bfloat16
PARTS = 2
BATCHES = (0, 1, 1, 3, 2, 3)
SCALED = (False, False, True, False, False, True)
LOTS = (0, 1, 2, 3, 0, 2)
FWD_UNITS, ROW_UNITS, GRAD_UNITS = (0, 4), (1, 3), (2, 5)
FAR_ROWS = (
    (0, 7, 0, 1),
    (1, 7, 1, 1),
    (0, 6, 0, 2),
    (0, 5, 0, -1),
    (1, 5, 1, -1),
    (1, 6, 1, -2),
)
FAR_STEPS = ((0, ((0, 1), (1, 1), (0, 2))), (4, ((0, -1), (1, -1), (1, -2))))

ORDER = (
    ("spread", 2),
    ("spread", 0),
    ("tables", 0),
    ("spread", 1),
    ("relay", 0, 1),
    ("relay", 0, 0),
    ("relay", 1, 0),
    ("finish", 0, 1),
    ("finish", 0, 0),
    ("relay", 1, 1),
    ("relay", 2, 1),
    ("relay", 2, 0),
    ("finish", 1, 0),
    ("collect", 0, 0),
    ("collect", 0, 1),
    ("finish", 1, 1),
    ("forward", 0),
    ("finish", 2, 0),
    ("collect", 1, 0),
    ("finish", 2, 1),
    ("back", 0, 0),
    ("collect", 2, 0),
    ("collect", 1, 1),
    ("back", 0, 1),
    ("spread", 3),
    ("collect", 2, 1),
    ("recompute", 1),
    ("far", 0, 0),
    ("backward", 1),
    ("far", 0, 1),
    ("back", 1, 1),
    ("near", 0, 0),
    ("back", 1, 0),
    ("near", 0, 1),
    ("far", 1, 1),
    ("far", 1, 0),
    ("own", 0),
    ("relay", 3, 0),
    ("near", 1, 1),
    ("near", 1, 0),
    ("relay", 3, 1),
    ("spread", 4),
    ("own", 1),
    ("finish", 3, 0),
    ("relay", 4, 0),
    ("relay", 4, 1),
    ("spread", 5),
    ("finish", 4, 1),
    ("finish", 4, 0),
    ("relay", 5, 1),
    ("collect", 4, 1),
    ("collect", 3, 0),
    ("relay", 5, 0),
    ("finish", 3, 1),
    ("collect", 4, 0),
    ("finish", 5, 1),
    ("forward", 2),
    ("finish", 5, 0),
    ("back", 2, 0),
    ("collect", 3, 1),
    ("collect", 5, 1),
    ("recompute", 3),
    ("back", 2, 1),
    ("collect", 5, 0),
    ("settle", 0),
    ("far", 2, 0),
    ("backward", 3),
    ("far", 2, 1),
    ("back", 3, 0),
    ("back", 3, 1),
    ("settle", 1),
    ("near", 2, 1),
    ("far", 3, 0),
    ("far", 3, 1),
    ("near", 2, 0),
    ("near", 3, 0),
    ("near", 3, 1),
    ("own", 2),
    ("own", 3),
)


def kernel(
    fwd_state,
    new_tokens,
    saved_input,
    grad_state,
    new_grads,
    norm_gain,
    w_gate,
    w_up,
    w_down,
    fwd_ids,
    fwd_gates,
    bwd_ids,
    bwd_gates,
    fwd_out,
    grad_out,
    inputs,
    gain,
    ids,
    gates,
    outs,
    input_sem,
    output_sem,
    gate_w,
    up_w,
    down_w,
    meta,
    table,
    held,
    cross,
    far,
    recv,
    partial,
    pair_in,
    results,
    cross_in,
    far_in,
    sums_in,
    sums_out,
    rows_in,
    fwd_gate,
    fwd_up,
    gate_pre,
    up_pre,
    hid_a,
    hid_b,
    stage,
    moved,
    grads,
    meta_send,
    meta_recv,
    row_send,
    row_recv,
    swap_send,
    swap_recv,
    pair_send,
    pair_recv,
    back_ssem,
    back_rsem,
    pipe_send,
    pipe_recv,
):
    pipe = lax.axis_index("pipe")
    sections = lax.axis_size("pipe")
    me = lax.axis_index("expert")
    chips = lax.axis_size("expert") // 2
    chip = me // 2
    core = me % 2
    ring = chips // 2
    column = chip // ring
    plane = chip % ring
    other = chip * 2 + 1 - core
    width = fwd_state.shape[-1]
    token_rows = fwd_state.shape[-2]
    topk = fwd_ids.shape[-2]
    slots = recv.shape[4]
    count = chips * slots
    hidden = gate_w.shape[1]
    wide = 256 if width // PARTS % 256 == 0 else width // PARTS
    after = lax.rem(pipe + 1, sections)
    before = lax.rem(pipe + sections - 1, sections)

    barrier = pltpu.get_barrier_semaphore()

    @pl.loop(1, chips)
    def _(j):
        peer = lax.rem(chip + j, chips) * 2 + core
        pl.semaphore_signal(barrier, inc=1, device_id={"expert": peer}, device_id_type=MESH)

    pl.semaphore_signal(barrier, inc=1, device_id={"expert": other}, device_id_type=MESH)
    pl.semaphore_signal(barrier, inc=1, device_id={"pipe": after}, device_id_type=MESH)
    pl.semaphore_signal(barrier, inc=1, device_id={"pipe": before}, device_id_type=MESH)

    sources = {
        "fwd_ids": (fwd_ids.at[:, 0], ids.at[0]),
        "fwd_gates": (fwd_gates.at[:, 0], gates.at[0]),
        "bwd_ids": (bwd_ids.at[:, 0], ids.at[1]),
        "bwd_gates": (bwd_gates.at[:, 0], gates.at[1]),
        "grad_state": (grad_state.at[0], held.at[2, 2]),
        "gain": (norm_gain, gain),
        "saved0": (saved_input.at[0, 0], inputs.at[2]),
        "fwd_state": (fwd_state.at[0], inputs.at[0]),
        "saved1": (saved_input.at[1, 0], inputs.at[3]),
        "gate": (w_gate.at[0], gate_w),
        "up": (w_up.at[0], up_w),
        "down": (w_down.at[0], down_w),
        "new_tokens": (new_tokens.at[0], inputs.at[1]),
        "new_grads": (new_grads.at[0], inputs.at[4]),
    }
    loads = {
        key: pltpu.make_async_copy(source, target, input_sem.at[i])
        for i, (key, (source, target)) in enumerate(sources.items())
    }
    for load in loads.values():
        load.start()

    def need(*keys):
        for key in keys:
            if key in loads:
                loads.pop(key).wait()

    def columns(i):
        return pl.ds(pl.multiple_of(i * wide, wide), wide)

    def part(half):
        return pl.ds(half * (width // PARTS), width // PARTS)

    def over_part(half):
        steps = width // PARTS // wide
        return pl.loop(half * steps, (half + 1) * steps, unroll=True)

    def device(across, step):
        to_column = lax.rem(column + across, 2)
        to_plane = lax.rem(plane + step + 2 * ring, ring)
        return (to_column * ring + to_plane) * 2 + core

    def expert(across, step):
        return device(across, step) // 2

    def remote(source, target, sends, receives, peer):
        return pltpu.make_async_remote_copy(
            src_ref=source,
            dst_ref=target,
            send_sem=sends,
            recv_sem=receives,
            device_id={"expert": peer},
            device_id_type=MESH,
        )

    def slot_weights(ids, gates):
        named = lax.broadcasted_iota(jnp.int32, (count, token_rows), 0) // slots
        place = lax.broadcasted_iota(jnp.int32, (count, token_rows), 0) % slots
        named = named.astype(F32)
        chosen = jnp.zeros((count, token_rows), F32)
        weight = jnp.zeros((count, token_rows), F32)
        for k in range(topk):
            hit = ids[k : k + 1] == named
            chosen = jnp.where(hit, 1.0, chosen)
            weight = jnp.where(hit, gates[k : k + 1], weight)
        row = lax.broadcasted_iota(jnp.int32, (token_rows, token_rows), 0)
        col = lax.broadcasted_iota(jnp.int32, (token_rows, token_rows), 1)
        earlier = jnp.where(row < col, 1.0, 0.0).astype(BF16)
        rank = jnp.dot(chosen.astype(BF16), earlier, preferred_element_type=F32)
        return jnp.where(rank == place.astype(F32), weight, 0.0)

    def inverse_rms(widened):
        return lax.rsqrt(jnp.mean(widened * widened, axis=-1, keepdims=True) + 1e-06)

    def normalize(values):
        widened = values.astype(F32)
        return (widened * inverse_rms(widened) * gain[...]).astype(BF16)

    meta_copies = [
        remote(meta.at[2], meta.at[2 - step], meta_send.at[i], meta_recv.at[i], device(0, step))
        for i, step in enumerate((1, -1, 2, -2))
    ]

    def first_hop(unit, half):
        return [
            remote(
                held.at[unit, 2, :, part(half)],
                held.at[unit, 2 - step, :, part(half)],
                row_send.at[unit, half, i],
                row_recv.at[unit, half, i],
                device(0, step),
            )
            for i, step in enumerate((1, -1))
        ]

    def second_hop(unit, half):
        return [
            remote(
                held.at[unit, 2 - step, :, part(half)],
                held.at[unit, 2 - 2 * step, :, part(half)],
                row_send.at[unit, half, 2 + i],
                row_recv.at[unit, half, 2 + i],
                device(0, step),
            )
            for i, step in enumerate((1, -1))
        ]

    def cross_copies(unit, half):
        return [
            remote(
                cross.at[LOTS[unit], slots_of, :, part(half)],
                recv.at[unit, core, 1, slots_of, :, part(half)],
                row_send.at[unit, half, 4 + i],
                row_recv.at[unit, half, 4 + i],
                device(1, 0),
            )
            for i, slots_of in enumerate((pl.ds(1, 3), pl.ds(0, 1), pl.ds(4, 1)))
        ]

    def far_copies(unit, half):
        return [
            remote(
                far.at[LOTS[unit], i, :, part(half)],
                recv.at[unit, core, to, slot, :, part(half)],
                row_send.at[unit, half, 7 + i],
                row_recv.at[unit, half, 7 + i],
                device(across, step),
            )
            for i, (to, slot, across, step) in enumerate(FAR_ROWS)
        ]

    def pick(unit, half, first, many, targets):
        share = len(targets) // many
        batch, scaled = BATCHES[unit], SCALED[unit]
        picked = jnp.concatenate(
            [table[batch, first + n // share, e] for n, (e, _) in enumerate(targets)], axis=0
        )
        scale = jnp.sum(picked, axis=1, keepdims=True)
        if many > 1:
            picked = jnp.concatenate([picked] * many, axis=1)
            row = lax.broadcasted_iota(jnp.int32, picked.shape, 0) // (share * slots)
            col = lax.broadcasted_iota(jnp.int32, picked.shape, 1) // token_rows
            picked = jnp.where(row == col, picked, 0.0)
        select = jnp.where(picked > 0.0, 1.0, 0.0).astype(BF16)

        @over_part(half)
        def _(i):
            cut = columns(i)
            block = held[unit, pl.ds(first, many), :, cut].reshape(many * token_rows, wide)
            rows = jnp.dot(select, block, preferred_element_type=F32)
            if scaled:
                rows = rows * scale
            for n, (_, target) in enumerate(targets):
                target[:, cut] = rows[n * slots : (n + 1) * slots].astype(BF16)

    def near(unit, slot):
        return [
            (expert(0, 0), recv.at[unit, core, 0, slot]),
            (expert(1, 0), cross.at[LOTS[unit], slot]),
        ]

    def spread(unit):
        for half in range(PARTS):
            for copy in first_hop(unit, half):
                copy.start()

    def relay(unit, half):
        arrivals, onward = first_hop(unit, half), second_hop(unit, half)
        for i in range(2):
            arrivals[i].wait_recv()
            onward[i].start()
        targets = [target for slot in (1, 2, 3) for target in near(unit, slot)]
        pick(unit, half, 1, 3, targets)
        cross_copies(unit, half)[0].start()

    def finish(unit, half):
        arrivals, beyond = second_hop(unit, half), far_copies(unit, half)
        crossing = cross_copies(unit, half)
        for i, (slot, steps) in enumerate(FAR_STEPS):
            arrivals[i].wait_recv()
            targets = [
                (expert(*at), far.at[LOTS[unit], 3 * i + n]) for n, at in enumerate(steps)
            ]
            pick(unit, half, slot, 1, targets)
            for n in range(3):
                beyond[3 * i + n].start()
        for i, slot in enumerate((0, 4)):
            pick(unit, half, slot, 1, near(unit, slot))
            crossing[1 + i].start()

    def release(unit):
        for half in range(PARTS):
            for copy in cross_copies(unit, half) + far_copies(unit, half):
                copy.wait_send()

    def swap_copy(unit, half, rail):
        half_rows = recv.at[unit, rail, :, :, :, part(half)]
        return remote(
            half_rows, half_rows, swap_send.at[unit, half], swap_recv.at[unit, half], other
        )

    def collect(unit, half):
        for copy in cross_copies(unit, half) + far_copies(unit, half):
            copy.wait_recv()
        swap_copy(unit, half, core).start()

    def gather(unit):
        for half in range(PARTS):
            swap_copy(unit, half, 1 - core).wait_recv()
            swap_copy(unit, half, core).wait_send()

            @over_part(half)
            def _(i):
                cut = columns(i)
                block = recv[unit, :, :, :, :, cut].astype(F32)
                rows_in[:, cut] = block.reshape(2 * count, wide).astype(BF16)

    def project(gate_to, up_to):
        @pl.loop(0, hidden // 256)
        def _(i):
            cut = pl.ds(pl.multiple_of(i * 256, 256), 256)
            gate_to[:, cut] = jnp.dot(rows_in[...], gate_w[:, cut], preferred_element_type=F32)
            up_to[:, cut] = jnp.dot(rows_in[...], up_w[:, cut], preferred_element_type=F32)

    def pair_copy(unit, half):
        return remote(
            partial.at[unit % 2, 1 - core, :, :, :, part(half)],
            pair_in.at[unit, :, :, :, part(half)],
            pair_send.at[unit, half],
            pair_recv.at[unit, half],
            other,
        )

    def result_copies(unit, half):
        straight = [
            remote(
                results.at[unit, to, slot, :, part(half)],
                far_in.at[unit, i, :, part(half)],
                back_ssem.at[unit, half, i],
                back_rsem.at[unit, half, i],
                device(across, -step),
            )
            for i, (to, slot, across, step) in enumerate(FAR_ROWS)
        ]
        crossing = [
            remote(
                results.at[unit, 1, slots_of, :, part(half)],
                cross_in.at[unit, slots_of, :, part(half)],
                back_ssem.at[unit, half, 6 + i],
                back_rsem.at[unit, half, 6 + i],
                device(1, 0),
            )
            for i, slots_of in enumerate((pl.ds(0, 1), pl.ds(4, 1), pl.ds(1, 3)))
        ]
        return straight + crossing

    def sum_copies(unit, half, hop):
        return [
            remote(
                sums_out.at[unit % 2, hop, i, :, part(half)],
                sums_in.at[unit, hop, i, :, part(half)],
                back_ssem.at[unit, half, 9 + 2 * hop + i],
                back_rsem.at[unit, half, 9 + 2 * hop + i],
                device(0, step),
            )
            for i, step in enumerate((-1, 1))
        ]

    def combine(unit, half, slot, terms, added, put):
        gated = unit % 2 == 0
        weights = jnp.transpose(
            jnp.concatenate([table[unit, slot, e] for e, _ in terms], axis=0)
        )
        if gated:
            high = weights.astype(BF16)
            low = (weights - high.astype(F32)).astype(BF16)
            matrix = jnp.concatenate([high, low], axis=0)
        else:
            matrix = jnp.where(weights > 0.0, 1.0, 0.0).astype(BF16)

        @over_part(half)
        def _(i):
            cut = columns(i)
            rows = jnp.concatenate([term[:, cut].astype(F32) for _, term in terms], axis=0)
            total = jnp.dot(matrix, rows.astype(BF16), preferred_element_type=F32)
            if gated:
                total = total[:token_rows] + total[token_rows:]
            for extra in added:
                total = total + extra[:, cut].astype(F32)
            put(cut, total)

    def close_terms(unit, slot):
        return [
            (expert(0, 0), results.at[unit, 0, slot]),
            (expert(1, 0), cross_in.at[unit, slot]),
        ]

    def sum_far(unit, half):
        onward = sum_copies(unit, half, 0)
        for copy in result_copies(unit, half)[:8]:
            copy.wait_recv()
        for i, (slot, steps) in enumerate(FAR_STEPS):
            terms = close_terms(unit, slot) + [
                (expert(*at), far_in.at[unit, 3 * i + n]) for n, at in enumerate(steps)
            ]
            target = sums_out.at[unit % 2, 0, i]

            def put(cut, total):
                target[:, cut] = total.astype(BF16)

            combine(unit, half, slot, terms, [], put)
            onward[i].start()

    def sum_near(unit, half):
        arrivals, onward = sum_copies(unit, half, 0), sum_copies(unit, half, 1)
        result_copies(unit, half)[8].wait_recv()
        for i, slot in enumerate((1, 3)):
            arrivals[i].wait_recv()
            target = sums_out.at[unit % 2, 1, i]

            def put(cut, total):
                target[:, cut] = total.astype(BF16)

            terms = close_terms(unit, slot)
            combine(unit, half, slot, terms, [sums_in.at[unit, 0, i]], put)
            onward[i].start()

    def sum_own(unit):
        def put(cut, total):
            stage[:, cut] = total

        added = [sums_in.at[unit, 1, i] for i in range(2)]
        for half in range(PARTS):
            for copy in sum_copies(unit, half, 1):
                copy.wait_recv()
            combine(unit, half, 2, close_terms(unit, 2), added, put)

    def sums_sent(unit):
        for half in range(PARTS):
            for hop in range(2):
                for copy in sum_copies(unit, half, hop):
                    copy.wait_send()

    def send_back(unit, half):
        pair_copy(unit, half).wait()

        @over_part(half)
        def _(i):
            cut = columns(i)
            mine = partial[unit % 2, core, :, :, :, cut].astype(F32)
            both = mine + pair_in[unit, :, :, :, cut].astype(F32)
            results[unit, :, :, :, cut] = both.astype(BF16)

        for copy in result_copies(unit, half):
            copy.start()

    def outputs(unit, rows):
        for half in range(PARTS):

            @over_part(half)
            def _(i):
                values = rows(columns(i)).reshape(2, 2, ring, slots, wide)
                partial[unit % 2, :, :, :, :, columns(i)] = values.astype(BF16)

            pair_copy(unit, half).start()

    def forward(unit):
        gather(FWD_UNITS[unit // 2])
        project(fwd_gate, fwd_up)
        gate = fwd_gate[...]
        hid_a[...] = (gate * jax.nn.sigmoid(gate) * fwd_up[...]).astype(BF16)
        outputs(
            unit, lambda cut: jnp.dot(hid_a[...], down_w[:, cut], preferred_element_type=F32)
        )

    def recompute(unit):
        gather(ROW_UNITS[unit // 2])
        project(gate_pre, up_pre)

    def backward(unit):
        gather(GRAD_UNITS[unit // 2])
        across = (((1,), (1,)), ((), ()))

        @pl.loop(0, hidden // 256)
        def _(i):
            cut = pl.ds(pl.multiple_of(i * 256, 256), 256)
            grad = lax.dot_general(rows_in[...], down_w[cut, :], across, preferred_element_type=F32)
            gate = gate_pre[:, cut]
            sigmoid = jax.nn.sigmoid(gate)
            hid_a[:, cut] = (
                grad * up_pre[:, cut] * sigmoid * (1.0 + gate * (1.0 - sigmoid))
            ).astype(BF16)
            hid_b[:, cut] = (grad * (gate * sigmoid)).astype(BF16)

        def rows(cut):
            total = lax.dot_general(
                hid_a[...], gate_w[cut, :], across, preferred_element_type=F32
            )
            return total + lax.dot_general(
                hid_b[...], up_w[cut, :], across, preferred_element_type=F32
            )

        outputs(unit, rows)

    def mixture(unit, base, target):
        sum_own(unit)
        target[...] = (base[...].astype(F32) + stage[...]).astype(BF16)

    def input_grad(unit, saved, cotangent, target):
        inverse = inverse_rms(saved.astype(F32))
        sum_own(unit)
        weighted = stage[...] * gain[...]
        widened = saved.astype(F32)
        correction = jnp.mean(weighted * widened, axis=-1, keepdims=True)
        target[...] = (
            cotangent[...].astype(F32)
            + inverse * weighted
            - widened * (inverse * inverse * inverse) * correction
        ).astype(BF16)

    def move(which, source, peer):
        return pltpu.make_async_remote_copy(
            src_ref=source,
            dst_ref=moved.at[which],
            send_sem=pipe_send.at[which],
            recv_sem=pipe_recv.at[which],
            device_id={"pipe": peer},
            device_id_type=MESH,
        )

    need("fwd_ids", "fwd_gates", "bwd_ids", "bwd_gates")
    for batch in range(4):
        begin = token_rows * batch
        meta[2, :topk, begin : begin + token_rows] = ids[batch % 2, batch // 2].astype(F32)
        meta[2, topk:, begin : begin + token_rows] = gates[batch % 2, batch // 2]
    current, cotangent = moved.at[0], moved.at[1]
    forth = move(0, outs.at[0], after)
    upward = move(1, grads, before)

    def begin_spread(unit):
        if unit == 0:
            need("fwd_state", "gain")
            held[0, 2] = normalize(inputs[0])
        elif unit == 1:
            need("saved0", "gain")
            held[1, 2] = normalize(inputs[2])
        elif unit == 2:
            need("grad_state")
        elif unit == 3:
            need("saved1", "gain")
            held[3, 2] = normalize(inputs[3])
        elif unit == 4:
            need("new_tokens")
            forth.wait()
            current[...] = jnp.where(pipe == 0, inputs[1], current[...])
            held[4, 2] = normalize(current[...])
            release(0)
            sums_sent(0)
        else:
            need("new_grads")
            upward.wait()
            cotangent[...] = jnp.where(pipe == sections - 1, inputs[4], cotangent[...])
            held[5, 2] = cotangent[...]
            release(2)
            sums_sent(1)
        spread(unit)

    def tables(_):
        for copy in meta_copies:
            copy.wait_recv()

        @pl.loop(0, 5)
        def _(slot):
            for batch in range(4):
                begin = token_rows * batch
                weights = slot_weights(
                    meta[slot, :topk, begin : begin + token_rows],
                    meta[slot, topk:, begin : begin + token_rows],
                )
                table[batch, slot] = weights.reshape(chips, slots, token_rows)

        need("gate", "up", "down")

    finals = [
        pltpu.make_async_copy(outs.at[i], target.at[0], output_sem.at[i])
        for i, target in enumerate((fwd_out, grad_out))
    ]

    def complete(unit):
        if unit == 0:
            mixture(0, inputs.at[0], outs.at[0])
            forth.start()
        elif unit == 1:
            input_grad(1, inputs[2], held.at[2, 2], grads)
            upward.start()
        elif unit == 2:
            mixture(2, current, outs.at[0])
            finals[0].start()
        else:
            input_grad(3, inputs[3], cotangent, outs.at[1])
            finals[1].start()

    pl.semaphore_wait(barrier, chips + 2)
    for copy in meta_copies:
        copy.start()
    def hops_sent(unit):
        for half in range(PARTS):
            for copy in first_hop(unit, half) + second_hop(unit, half):
                copy.wait_send()

    def results_sent(unit):
        for half in range(PARTS):
            for copy in result_copies(unit, half):
                copy.wait_send()

    def settle(stage):
        if stage == 0:
            for copy in meta_copies:
                copy.wait_send()
            for unit in range(4):
                hops_sent(unit)
            for unit in (1, 3):
                release(unit)
            for unit in (0, 1):
                results_sent(unit)
        elif stage == 1:
            for unit in (4, 5):
                hops_sent(unit)
                release(unit)
        else:
            for unit in (2, 3):
                results_sent(unit)
                sums_sent(unit)

    steps = {
        "settle": settle,
        "spread": begin_spread,
        "tables": tables,
        "relay": relay,
        "finish": finish,
        "collect": collect,
        "forward": forward,
        "recompute": recompute,
        "backward": backward,
        "back": send_back,
        "far": sum_far,
        "near": sum_near,
        "own": complete,
    }
    for name, *which in ORDER:
        steps[name](*which)
    settle(2)
    for copy in finals:
        copy.wait()


def hand_over(first, second, first_out, second_out, held, in_sems, out_sems):
    pairs = enumerate(((first, first_out), (second, second_out)))
    arrive, leave = [], []
    for i, (source, target) in pairs:
        for half in range(PARTS):
            size = held.shape[-1] // PARTS
            cut = pl.ds(half * size, size)
            between = held.at[i, :, :, cut]
            arrive.append(
                pltpu.make_async_copy(source.at[:, :, cut], between, in_sems.at[i, half])
            )
            leave.append(
                pltpu.make_async_copy(between, target.at[:, :, cut], out_sems.at[i, half])
            )
    for copy in arrive:
        copy.start()
    for before, after in zip(arrive, leave):
        before.wait()
        after.start()
    for copy in leave:
        copy.wait()


def shards(*arrays):
    fwd_state, fwd_ids, w_gate = arrays[0], arrays[9], arrays[6]
    token_rows, width = fwd_state.shape[1:]
    hidden = w_gate.shape[2]
    chips = lax.axis_size("expert") // 2
    topk = fwd_ids.shape[3]
    slots = token_rows * topk // chips
    count = 2 * chips * slots
    dma = pltpu.SemaphoreType.DMA
    hbm = pl.BlockSpec(memory_space=pl.ANY)
    row = jax.ShapeDtypeStruct(fwd_state.shape, BF16)
    routes = [jnp.transpose(array, (0, 1, 3, 2)) for array in arrays[9:]]
    results = pl.pallas_call(
        kernel,
        out_shape=(row, row),
        in_specs=[hbm] * len(arrays),
        out_specs=(hbm, hbm),
        scratch_shapes=[
            pltpu.VMEM((5, token_rows, width), BF16),
            pltpu.VMEM((1, width), F32),
            pltpu.VMEM((2, 2, topk, token_rows), jnp.int32),
            pltpu.VMEM((2, 2, topk, token_rows), F32),
            pltpu.VMEM((2, token_rows, width), BF16),
            dma((14,)),
            dma((2,)),
            pltpu.VMEM((width, hidden), BF16),
            pltpu.VMEM((width, hidden), BF16),
            pltpu.VMEM((hidden, width), BF16),
            pltpu.VMEM((5, 2 * topk, 4 * token_rows), F32),
            pltpu.VMEM((4, 5, chips, slots, token_rows), F32),
            pltpu.VMEM((6, 5, token_rows, width), BF16),
            pltpu.VMEM((4, 5, slots, width), BF16),
            pltpu.VMEM((4, 6, slots, width), BF16),
            pltpu.VMEM((6, 2, 2, chips // 2, slots, width), BF16),
            pltpu.VMEM((2, 2, 2, chips // 2, slots, width), BF16),
            pltpu.VMEM((4, 2, chips // 2, slots, width), BF16),
            pltpu.VMEM((4, 2, chips // 2, slots, width), BF16),
            pltpu.VMEM((4, 5, slots, width), BF16),
            pltpu.VMEM((4, 6, slots, width), BF16),
            pltpu.VMEM((4, 2, 2, token_rows, width), BF16),
            pltpu.VMEM((2, 2, 2, token_rows, width), BF16),
            pltpu.VMEM((count, width), BF16),
            pltpu.VMEM((count, hidden), F32),
            pltpu.VMEM((count, hidden), F32),
            pltpu.VMEM((count, hidden), F32),
            pltpu.VMEM((count, hidden), F32),
            pltpu.VMEM((count, hidden), BF16),
            pltpu.VMEM((count, hidden), BF16),
            pltpu.VMEM((token_rows, width), F32),
            pltpu.VMEM((2, token_rows, width), BF16),
            pltpu.VMEM((token_rows, width), BF16),
            dma((4,)),
            dma((4,)),
            dma((6, PARTS, 13)),
            dma((6, PARTS, 13)),
            dma((6, PARTS)),
            dma((6, PARTS)),
            dma((4, PARTS)),
            dma((4, PARTS)),
            dma((4, PARTS, 13)),
            dma((4, PARTS, 13)),
            dma((2,)),
            dma((2,)),
        ],
        compiler_params=pltpu.CompilerParams(
            collective_id=0, has_side_effects=True, vmem_limit_bytes=60 * 2**20
        ),
        name="relay",
    )(*arrays[:9], *routes)
    return pl.pallas_call(
        hand_over,
        out_shape=(row, row),
        in_specs=[hbm] * 2,
        out_specs=(hbm, hbm),
        scratch_shapes=[
            pltpu.VMEM((2, *fwd_state.shape), BF16),
            dma((2, PARTS)),
            dma((2, PARTS)),
        ],
        name="hand_over",
    )(*results)


def solution(mesh):
    placed = (
        P("pipe", "expert", None),
        P(None, "expert", None),
        P(None, "pipe", "expert", None),
        P("pipe", "expert", None),
        P(None, "expert", None),
        P("pipe", None),
        P("pipe", None, "expert"),
        P("pipe", None, "expert"),
        P("pipe", "expert", None),
        P(None, "pipe", "expert", None),
        P(None, "pipe", "expert", None),
        P(None, "pipe", "expert", None),
        P(None, "pipe", "expert", None),
    )
    return jax.shard_map(
        shards,
        mesh=mesh,
        in_specs=placed,
        out_specs=(P("pipe", "expert", None), P("pipe", "expert", None)),
        check_vma=False,
    )
```
